32 devices in a mesh: batch: 8 (over y, x, core), seq: 4 (over z).
Axes of the slice: x: 2, y: 2, z: 4, core: 2. Of those that a mesh axis runs over, the one named last changes fastest.
Arguments:
- layer_input: bfloat16 [8, 2048, 768], P('batch', 'seq'), may hold values from -6 to 6
- segment_ids: int32 [8, 2048], P('batch', 'seq'), may hold values from 0 to 16, as said below
- w_qkv: bfloat16 [768, 2304], replicated, may hold values from -0.21875 to 0.21875
- b_query: float32 [768], replicated, may hold values from -1.8 to 1.8
- b_value: float32 [768], replicated, may hold values from -1.8 to 1.8
- w_out: bfloat16 [768, 768], replicated, may hold values from -0.875 to 0.875
- b_out: float32 [768], replicated, may hold values from -1.8 to 1.8
- ln1_gain: float32 [768], replicated, may hold values from 0.5 to 1.5
- ln1_bias: float32 [768], replicated, may hold values from -1.8 to 1.8
- w_up: bfloat16 [768, 3072], replicated, may hold values from -0.21875 to 0.21875
- b_up: float32 [3072], replicated, may hold values from -1.8 to 1.8
- w_down: bfloat16 [3072, 768], replicated, may hold values from -0.109375 to 0.109375
- b_down: float32 [768], replicated, may hold values from -1.8 to 1.8
- ln2_gain: float32 [768], replicated, may hold values from 0.5 to 1.5
- ln2_bias: float32 [768], replicated, may hold values from -1.8 to 1.8
- cotangent: bfloat16 [8, 2048, 768], P('batch', 'seq'), may hold values from -6 to 6
Outputs:
- out: bfloat16 [8, 2048, 768], P('batch', 'seq')
- d_x: float32 [8, 2048, 768], P('batch', 'seq')
- d_w_qkv: float32 [768, 2304], replicated
- d_b_query: float32 [768], replicated
- d_b_value: float32 [768], replicated
- d_w_out: float32 [768, 768], replicated
- d_b_out: float32 [768], replicated
- d_ln1_gain: float32 [768], replicated
- d_ln1_bias: float32 [768], replicated
- d_w_up: float32 [768, 3072], replicated
- d_b_up: float32 [3072], replicated
- d_w_down: float32 [3072, 768], replicated
- d_b_down: float32 [768], replicated
- d_ln2_gain: float32 [768], replicated
- d_ln2_bias: float32 [768], replicated
The draws below stay inside these ranges and needn't reach their ends.
Inputs may be any that keep to these rules, and one draw needn't show every extreme that they name: `segment_ids`: along each stream the segment ids never fall; a document is a run of equal ids and attends only within itself. In each batch index one of its 1 streams, which one drawn, holds a document from a position below 512 to one at or past 2048 - 512.
All inputs are finite; a program needn't handle non-finite values.
Results may differ from the reference program's by a relative error of at most 0.035.
Values may be sent and summed in bfloat16 or wider, within the bound.
No kernel may reach another device: no remote copies, remote signals or barrier semaphores. Data moves between devices by JAX's collectives and lax.ppermute only.
A program may use at most 256 MiB of HBM per device.

```python
import math
import jax
import jax.numpy as jnp
from jax import lax

D = 768
HEADS = 12
FF = 3072
SPB = 1
SHARD = 512
MINDOC = 128
HEAD_DIM = 64
L = 2048
STREAMS = 8


def draw_segment_ids(key, part):
    key_pick, key_len, key_first, key_last = jax.random.split(jax.random.fold_in(key, 7), 4)
    count = L // MINDOC + 1
    top_id = L // MINDOC
    lengths = jax.random.randint(key_len, (STREAMS, count), MINDOC, 3 * SHARD)
    ends = jnp.cumsum(lengths, axis=1)
    positions = jnp.arange(L, dtype=jnp.int32)
    drawn = jnp.sum((ends[:, None, :] <= positions[None, :, None]).astype(jnp.int32), axis=2)
    drawn = drawn + (top_id - drawn[:, -1:])
    first = jax.random.randint(key_first, (STREAMS,), MINDOC, SHARD)
    last = jax.random.randint(key_last, (STREAMS,), MINDOC, SHARD)
    spanning = (positions[None, :] >= first[:, None]).astype(jnp.int32) + (positions[None, :] >= (L - last)[:, None]).astype(jnp.int32)
    spanning = jnp.where(spanning == 2, top_id, spanning)
    picked = jax.random.randint(key_pick, (STREAMS // SPB,), 0, SPB)
    chosen = jnp.arange(STREAMS, dtype=jnp.int32) % SPB == jnp.repeat(picked, SPB)
    return jnp.where(chosen[:, None], spanning, drawn).astype(jnp.int32)


def shard_levels(stream_key, dims, pieces, low, largest):
    level = 1.0
    for position, parts in pieces:
        draws = jax.random.uniform(jax.random.fold_in(jax.random.fold_in(stream_key, 6), position), (parts,), jnp.float32, low / len(pieces), largest / len(pieces))
        level = level * jnp.repeat(jnp.exp(draws), dims[position] // parts).reshape((-1,) + (1,) * (len(dims) - 1 - position))
    return level


def gaussian(key, dims, scale, reach, pieces=(), held_as=jnp.bfloat16):
    values = scale * jax.random.normal(key, dims, jnp.float32)
    if pieces:
        values = values * shard_levels(key, dims, pieces, -0.22, 0.18)
    return jnp.clip(values, -reach, reach).astype(held_as)


def setup_inputs(seed: int = 0) -> dict:
    seeds = jax.random.split(jax.random.key(seed), 17)
    layer_input = gaussian(seeds[0], (STREAMS, L, D), 1.0, 6.0, ((0, 8), (1, 4)))
    segment_ids = draw_segment_ids(jax.random.fold_in(seeds[16], 71), 0)
    w_qkv = gaussian(seeds[2], (D, 3 * D), D ** -0.5, 0.21875)
    b_query = gaussian(seeds[3], (D,), 0.3, 1.8, (), jnp.float32)
    b_value = gaussian(seeds[4], (D,), 0.3, 1.8, (), jnp.float32)
    w_out = gaussian(seeds[5], (D, D), (D // 16) ** -0.5, 0.875)
    b_out = gaussian(seeds[6], (D,), 0.3, 1.8, (), jnp.float32)
    ln1_gain = jnp.clip(1.0 + 0.1 * jax.random.normal(seeds[7], (D,), jnp.float32), 0.5, 1.5)
    ln1_bias = gaussian(seeds[8], (D,), 0.3, 1.8, (), jnp.float32)
    w_up = gaussian(seeds[9], (D, FF), D ** -0.5, 0.21875)
    b_up = gaussian(seeds[10], (FF,), 0.3, 1.8, (), jnp.float32)
    w_down = gaussian(seeds[11], (FF, D), FF ** -0.5, 0.109375)
    b_down = gaussian(seeds[12], (D,), 0.3, 1.8, (), jnp.float32)
    ln2_gain = jnp.clip(1.0 + 0.1 * jax.random.normal(seeds[13], (D,), jnp.float32), 0.5, 1.5)
    ln2_bias = gaussian(seeds[14], (D,), 0.3, 1.8, (), jnp.float32)
    cotangent = gaussian(seeds[15], (STREAMS, L, D), 1.0, 6.0, ((0, 8), (1, 4)))
    return {"layer_input": layer_input, "segment_ids": segment_ids, "w_qkv": w_qkv, "b_query": b_query, "b_value": b_value, "w_out": w_out, "b_out": b_out, "ln1_gain": ln1_gain, "ln1_bias": ln1_bias, "w_up": w_up, "b_up": b_up, "w_down": w_down, "b_down": b_down, "ln2_gain": ln2_gain, "ln2_bias": ln2_bias, "cotangent": cotangent}


@jax.custom_vjp
def low(v):
    return lax.optimization_barrier(v.astype(jnp.bfloat16)).astype(jnp.float32)

@jax.custom_vjp
def low_back(v):
    return v

def low_keep(v):
    return (low(v), None)

def low_pass(kept, grad):
    return (grad,)

def back_keep(v):
    return (v, None)

def back_low(kept, grad):
    return (low(grad),)
low.defvjp(low_keep, low_pass)
low_back.defvjp(back_keep, back_low)

def product(left, right):
    return jnp.dot(left, right, precision=lax.Precision.HIGHEST, preferred_element_type=jnp.float32)

def layer_norm(hidden, gain, shift):
    centred = hidden - lax.optimization_barrier(jnp.mean(hidden, axis=-1, keepdims=True))
    scaled = centred * lax.rsqrt(lax.optimization_barrier(jnp.mean(centred * centred, axis=-1, keepdims=True)) + 1e-05)
    return scaled * gain + shift

def gelu_tanh(value):
    return jax.nn.gelu(value, approximate=True)

def attend(queries, keys, values, ids):
    length = queries.shape[0]
    size = math.gcd(length, 512)
    scale = HEAD_DIM ** (-0.5)
    query_blocks = queries.reshape(length // size, size, HEADS, HEAD_DIM)
    id_blocks = ids.reshape(length // size, size)

    def block(items):
        query_block, id_block = items
        raw = jnp.einsum('qhd,khd->hqk', query_block, keys, precision=lax.Precision.HIGHEST)
        scores = low_back(raw) * scale
        allowed = (id_block[:, None] == ids[None, :])[None]
        scores = jnp.where(allowed, scores, -1e+30)
        probs = jax.nn.softmax(scores, axis=-1)
        return jnp.einsum('hqk,khd->qhd', low(probs), values, precision=lax.Precision.HIGHEST)
    result = lax.map(jax.checkpoint(block), (query_blocks, id_blocks))
    return result.reshape(length, HEADS * HEAD_DIM)

def layer(params, inputs, ids):
    w_qkv, b_query, b_value, w_out, b_out, gain_one, shift_one, w_up, b_up, w_down, b_down, gain_two, shift_two = params
    width = inputs.shape[1]
    mixed = low_back(product(low(inputs), w_qkv))
    queries = low(mixed[:, :width] + b_query)
    keys = low(mixed[:, width:2 * width])
    values = low(mixed[:, 2 * width:] + b_value)
    rows = inputs.shape[0]
    attended = attend(queries.reshape(rows, HEADS, HEAD_DIM), keys.reshape(rows, HEADS, HEAD_DIM), values.reshape(rows, HEADS, HEAD_DIM), ids)
    attended = low(low_back(attended))
    first = inputs + low_back(product(attended, w_out)) + b_out
    normed = layer_norm(first, gain_one, shift_one)
    hidden = low_back(product(low(normed), w_up)) + b_up
    activated = low(gelu_tanh(hidden))
    second = normed + low_back(product(activated, w_down)) + b_down
    return layer_norm(second, gain_two, shift_two)

def reference(layer_input, segment_ids, w_qkv, b_query, b_value, w_out, b_out, ln1_gain, ln1_bias, w_up, b_up, w_down, b_down, ln2_gain, ln2_bias, cotangent):
    params = tuple((p.astype(jnp.float32) for p in (w_qkv, b_query, b_value, w_out, b_out, ln1_gain, ln1_bias, w_up, b_up, w_down, b_down, ln2_gain, ln2_bias)))

    def stream(carry, item):
        inputs, ids, grad = item

        def forward(pp, xx):
            return layer(pp, xx, ids)
        result, pull = jax.vjp(forward, params, inputs.astype(jnp.float32))
        d_params, d_inputs = pull(grad.astype(jnp.float32))
        carry = jax.tree.map(jnp.add, carry, d_params)
        return (carry, (result.astype(jnp.bfloat16), d_inputs))
    zeros = jax.tree.map(jnp.zeros_like, params)
    sums, (out, d_x) = lax.scan(stream, zeros, (layer_input, segment_ids, cotangent))
    return (out, d_x, sums[0], sums[1], sums[2], sums[3], sums[4], sums[5], sums[6], sums[7], sums[8], sums[9], sums[10], sums[11], sums[12])
```

```python
import functools
import math

import jax
import jax.numpy as jnp
from jax import lax
from jax.experimental import pallas as pl
from jax.experimental.pallas import tpu as pltpu
from jax.sharding import PartitionSpec as P

HEADS = 12
LANES = 128
MASK = 1e30
BF = jnp.bfloat16
F32 = jnp.float32
VMEM = 56 * 2**20
EXTRA = 128


def dot(left, right, contract=((1,), (0,))):
    return lax.dot_general(left, right, (contract, ((), ())), preferred_element_type=F32)


def stages_of(axis):
    return [(axis, bit) for bit in range(int(math.log2(lax.axis_size(axis))))]


def bit_of(stage):
    index = lax.axis_index(stage[0])
    if len(stage) == 2:
        return (index >> stage[1]) & 1
    return jnp.where(index % 2 == 0, index >> stage[1], index >> stage[2]) & 1


def swap(value, stage):
    count = lax.axis_size(stage[0])
    bits = stage[1:] * 2
    return lax.ppermute(value, stage[0], [(i, i ^ (1 << bits[i % 2])) for i in range(count)])


ANYWHERE = pl.BlockSpec(memory_space=pl.ANY)


def together(values, late=()):
    if len(values) + len(late) < 2:
        return list(values)
    return pl.pallas_call(
        lambda *refs: None,
        in_specs=[ANYWHERE] * (len(values) + len(late)),
        out_specs=[ANYWHERE] * len(values),
        out_shape=[jax.ShapeDtypeStruct(v.shape, v.dtype) for v in values],
        input_output_aliases={i: i for i in range(len(values))},
        name="together",
    )(*values, *late)


def part_of(terms, index, parts):
    rows = terms[0].shape[0] // parts
    total = lax.dynamic_slice_in_dim(terms[0], index * rows, rows, 0)
    if len(terms) == 1:
        return total
    total = total.astype(F32)
    for term in terms[1:]:
        total = total + lax.dynamic_slice_in_dim(term, index * rows, rows, 0).astype(F32)
    return total.astype(BF)


def rest_of(terms, stage, came):
    mine = bit_of(stage)
    rows = terms[0].shape[0] // 2
    return [lax.dynamic_slice_in_dim(t, mine * rows, rows, 0) for t in terms] + [came]


def split(value):
    half = value.shape[0] // 2
    return value[:half], value[half:]


def total_of(terms):
    total = terms[0].astype(F32)
    for term in terms[1:]:
        total = total + term.astype(F32)
    return total.astype(BF)


def joined(mine, other, stage):
    return jnp.where(
        bit_of(stage) == 0,
        jnp.concatenate([mine, other], axis=0),
        jnp.concatenate([other, mine], axis=0),
    )


def sum_everywhere(terms):
    core, chips = stages_of("batch")[0], stages_of("batch")[1:]
    plane = [(axis, one, two) for (axis, one), (_, two) in zip(chips, chips[::-1])]
    order = plane + stages_of("seq")
    for stage in order:
        came, _ = yield part_of(terms, 1 - bit_of(stage), 2), stage
        terms = rest_of(terms, stage, came)
    value = total_of(terms)
    for stage in order[::-1]:
        came, value = yield value, stage
        value = joined(value, came, stage)
    came, value = yield value, core
    return value, came


def line_scatter(sent):
    stages = stages_of("seq")
    came, kept = yield sent, stages[0]
    for axis, bit in stages[1:]:
        value = kept + came.astype(F32)
        mine = (lax.axis_index(axis) >> bit) & 1
        pairs = value.reshape(value.shape[0] // 2, 2, *value.shape[1:])
        sent = lax.dynamic_index_in_dim(pairs, 1 - mine, 1, keepdims=False).astype(BF)
        kept = lax.dynamic_index_in_dim(pairs, mine, 1, keepdims=False)
        if bit + 1 < len(stages):
            came, _ = yield sent, (axis, bit)
    parts = []
    for part in split(sent[0]):
        parts.append((yield part, stages[-1])[0])
    return kept[0] + jnp.concatenate(parts, axis=0).astype(F32)


class Exchanges:
    def __init__(self):
        self.chains, self.came, self.sent, self.results = {}, {}, {}, {}

    def add(self, name, chain):
        self.chains[name] = chain

    def go(self, names, late=(), kept=None, land=()):
        names = [n for n in names if n not in self.results]
        waiting = [n for n in names if n in self.came]
        landing = waiting + list(land)
        if landing:
            self.came.update(zip(landing, together([self.came[n] for n in landing], late)))
        next_sent, stages = {}, {}
        for name in names:
            try:
                if name not in waiting:
                    next_sent[name], stages[name] = next(self.chains[name])
                    continue
                back = self.sent[name]
                if name == "input" and kept is not None:
                    back = kept
                next_sent[name], stages[name] = self.chains[name].send((self.came[name], back))
            except StopIteration as stop:
                self.results[name] = stop.value
        next_sent = dict(zip(next_sent, together(list(next_sent.values()))))
        for name, value in next_sent.items():
            self.sent[name], self.came[name] = value, swap(value, stages[name])
        return list(next_sent.values())


def line_steps(block):
    count = lax.axis_size("seq")
    pairs = [
        [(i, i ^ 1) for i in range(count)],
        [(i, ((i + 1) ^ 1) - 1) for i in range(1, count - 1)],
    ]
    one = two = block
    for k in range(1, count):
        one, two = lax.ppermute(two, "seq", pairs[0]), lax.ppermute(one, "seq", pairs[1])
        late = yield
        one, two = together([one, two], late)
        yield one, two


def whole_spec(shape):
    return pl.BlockSpec(shape, lambda *_: (0,) * len(shape))


def params(flops, nbytes):
    return dict(
        compiler_params=pltpu.CompilerParams(vmem_limit_bytes=VMEM),
        cost_estimate=pl.CostEstimate(flops=flops, bytes_accessed=nbytes, transcendentals=0),
    )


def hot(ids_row, same, other):
    spread = jnp.broadcast_to(ids_row.astype(F32), (LANES, ids_row.shape[1]))
    lanes = lax.broadcasted_iota(jnp.int32, spread.shape, 0).astype(F32)
    return jnp.transpose(jnp.where(spread == lanes, same, other)).astype(BF)


def project_kernel(first, rows, place_ref, *refs):
    refs = list(refs)
    blocks = [refs.pop(0) for _ in range(1 if first else 2)]
    w_refs = [refs.pop(0) for _ in range(3 if first else 2)]
    b_refs = [refs.pop(0) for _ in range(3 if first else 2)]
    refs = refs if first else refs[2:]
    whole_ref, kv_ref = refs.pop(0), refs.pop(0)
    if first:
        q_ref, qh_ref = refs.pop(0), refs.pop(0)
    token_ref, key_hot, mixed, sems = refs
    token_ref[...] = jnp.zeros_like(token_ref)
    width = blocks[0].shape[1]
    step = pl.program_id(0)
    last = pl.num_programs(0) - 1
    lanes = mixed.shape[-1]

    def valid(b):
        return place_ref[2 + b] == 1

    def block_copies(b):
        at = pl.ds(place_ref[b] * rows, rows)
        return [
            pltpu.make_async_copy(blocks[b].at[pl.ds(0, rows)], whole_ref.at[at], sems.at[b, 0]),
            pltpu.make_async_copy(
                key_hot.at[b], kv_ref.at[at, pl.ds(2 * width, LANES)], sems.at[b, 1]
            ),
        ]

    def step_copies(b, at_step):
        at = pl.ds(place_ref[b] * rows, rows)
        begin = pl.multiple_of(at_step * lanes, LANES)
        return [
            pltpu.make_async_copy(
                mixed.at[b, i, at_step], kv_ref.at[at, pl.ds(i * width + begin, lanes)],
                sems.at[b, 2 + i],
            )
            for i in range(2)
        ]

    for b in range(len(blocks)):

        @pl.when(jnp.logical_and(step == 0, valid(b)))
        def _():
            ids = blocks[b][rows : rows + 16, :rows][0:1]
            key_hot[b] = hot(ids, 0.0, 1.0)
            if first:
                qh_ref[...] = hot(ids, -MASK, 0.0)
            for copy in block_copies(b):
                copy.start()

        @pl.when(valid(b))
        def _():
            block = blocks[b][:rows]
            for i in range(2):
                mixed[b, i, step] = (dot(block, w_refs[i][...]) + b_refs[i][...]).astype(BF)
            if first:
                q_ref[...] = (dot(block, w_refs[2][...]) + b_refs[2][...]).astype(BF)

        @pl.when(jnp.logical_and(step > 0, valid(b)))
        def _():
            for copy in step_copies(b, step - 1):
                copy.wait()

        @pl.when(valid(b))
        def _():
            for copy in step_copies(b, step):
                copy.start()

        @pl.when(jnp.logical_and(step == last, valid(b)))
        def _():
            for copy in step_copies(b, step) + block_copies(b):
                copy.wait()


def project(first, place, blocks, w_qkv, bias, state, length):
    width = w_qkv.shape[0]
    rows = blocks[0].shape[0] - 16
    lanes = 2 * LANES
    steps = width // lanes
    full = whole_spec

    def columns(count, which):
        return pl.BlockSpec((count, lanes), lambda p, *_: (0, which * steps + p))

    parts = (1, 2, 0) if first else (1, 2)
    in_specs = [full(blocks[0].shape)] * len(blocks)
    in_specs += [columns(width, i) for i in parts] + [columns(1, i) for i in parts]
    operands = [*blocks] + [w_qkv] * len(parts) + [bias] * len(parts)
    out_specs = [ANYWHERE, ANYWHERE]
    out_shape = [
        jax.ShapeDtypeStruct((length, width), BF),
        jax.ShapeDtypeStruct((length, 2 * width + LANES), BF),
    ]
    aliases = {}
    if first:
        out_specs += [pl.BlockSpec((rows, lanes), lambda p, *_: (0, p)), full((rows, LANES))]
        out_shape += [
            jax.ShapeDtypeStruct((rows, width), BF),
            jax.ShapeDtypeStruct((rows, LANES), BF),
        ]
    else:
        in_specs += [ANYWHERE, ANYWHERE]
        operands += state
        aliases = {len(operands) - 1: 0, len(operands): 1}
    out_specs.append(full((8, LANES)))
    out_shape.append(jax.ShapeDtypeStruct((8, LANES), F32))
    return pl.pallas_call(
        functools.partial(project_kernel, first, rows),
        grid_spec=pltpu.PrefetchScalarGridSpec(
            num_scalar_prefetch=1,
            grid=(steps,),
            in_specs=in_specs,
            out_specs=out_specs,
            scratch_shapes=[
                pltpu.VMEM((len(blocks), rows, LANES), BF),
                pltpu.VMEM((len(blocks), 2, steps, rows, lanes), BF),
                pltpu.SemaphoreType.DMA((len(blocks), 4)),
            ],
        ),
        out_shape=out_shape,
        input_output_aliases=aliases,
        name="project",
        **params(2 * len(blocks) * rows * width * width, 8 * rows * width),
    )(place, *operands)


def attend_kernel(scale, tile, q_ref, k_ref, v_ref, qh_ref, kh_ref, o_ref, low_ref, lse_ref):
    half = LANES // 2
    lane = lax.broadcasted_iota(jnp.int32, (1, LANES), 1)
    lower = lane < half
    factor = scale * math.log2(math.e)
    jobs = [(t, h) for t in range(q_ref.shape[0] // tile) for h in range(2)]

    def scores_of(t, h):
        at = slice(t * tile, (t + 1) * tile)
        query = q_ref[at]
        query = jnp.where(lane // half == h, query, jnp.zeros_like(query))
        query = jnp.concatenate([query, qh_ref[at]], axis=1)
        return dot(query, jnp.concatenate([k_ref[...], kh_ref[...]], axis=1), ((1,), (1,)))

    ready = scores_of(*jobs[0])
    before = None
    for i, (t, h) in enumerate(jobs):
        scores = ready
        if i + 1 < len(jobs):
            ready = scores_of(*jobs[i + 1])
        peak = jnp.max(scores, axis=1, keepdims=True)
        weights = jnp.exp2((scores - peak) * factor).astype(BF)
        value = v_ref[...]
        both = dot(weights, jnp.concatenate([value, jnp.ones_like(value)], axis=1))
        total = both[:, LANES:]
        now = both[:, :LANES] / total, peak * factor + jnp.log2(total)
        if h == 0:
            before = now
            continue
        at = slice(t * tile, (t + 1) * tile)
        out = jnp.where(lower, before[0], now[0])
        o_ref[at] = out
        low_ref[at] = out.astype(BF)
        turned = jnp.transpose(jnp.where(lower, before[1], now[1]))
        lse_ref[0, :, at] = jnp.concatenate([turned[0:4], turned[half : half + 4]], axis=0)


def attend(queries, keys_values, query_hot, scale):
    rows, width = queries.shape
    length = keys_values.shape[0]
    pairs = width // LANES
    by_pair = pl.BlockSpec((rows, LANES), lambda p: (0, p))
    return pl.pallas_call(
        functools.partial(attend_kernel, scale, 256),
        grid=(pairs,),
        in_specs=[
            by_pair,
            pl.BlockSpec((length, LANES), lambda p: (0, p)),
            pl.BlockSpec((length, LANES), lambda p: (0, pairs + p)),
            pl.BlockSpec((rows, LANES), lambda p: (0, 0)),
            pl.BlockSpec((length, LANES), lambda p: (0, 2 * pairs)),
        ],
        out_specs=[by_pair, by_pair, pl.BlockSpec((1, 8, rows), lambda p: (p, 0, 0))],
        out_shape=[
            jax.ShapeDtypeStruct((rows, width), F32),
            jax.ShapeDtypeStruct((rows, width), BF),
            jax.ShapeDtypeStruct((pairs, 8, rows), F32),
        ],
        name="attend",
        **params(4 * rows * length * width, 8 * length * width),
    )(queries, keys_values, keys_values, query_hot, keys_values)


def attend_back_kernel(
    final, scale, pairs, skip, at_ref, q_ref, k_ref, v_ref, qh_ref, kh_ref, do_ref, o_ref,
    lse_ref, *refs,
):
    refs = list(refs)
    if final:
        dq_in, sums_in = refs.pop(0), refs.pop(0)
    dq_ref, sums_ref, dk_ref, dv_ref, token_ref, dq_acc, delta_acc, sv_acc = refs[skip:]
    step = pl.program_id(1)
    half = LANES // 2
    lane = lax.broadcasted_iota(jnp.int32, (1, LANES), 1)
    factor = scale * math.log2(math.e)
    token_ref[...] = jnp.zeros_like(token_ref)

    @pl.when(step == 0)
    def _():
        if final:
            dq_acc[...] = dq_in[...]
            sv_acc[...] = sums_in[...]
        else:
            dq_acc[...] = jnp.zeros_like(dq_acc)
            sv_acc[...] = jnp.zeros_like(sv_acc)
        for p in range(pairs):
            at = slice(p * LANES, (p + 1) * LANES)
            both = jnp.transpose(do_ref[:, at].astype(F32) * o_ref[:, at])
            delta_acc[p, 0:1] = jnp.sum(both[:half], axis=0, keepdims=True)
            delta_acc[p, 1:2] = jnp.sum(both[half:], axis=0, keepdims=True)

    jobs = [(p, h) for p in range(pairs) for h in range(2)]

    def products(p, h):
        at = slice(p * LANES, (p + 1) * LANES)
        own = lane // half == h
        query, d_out = q_ref[:, at], do_ref[:, at]
        query = jnp.where(own, query, jnp.zeros_like(query))
        d_out = jnp.where(own, d_out, jnp.zeros_like(d_out))
        keys = jnp.concatenate([k_ref[:, at], kh_ref[...]], axis=1)
        scores = dot(keys, jnp.concatenate([query, qh_ref[...]], axis=1), ((1,), (1,)))
        return scores, dot(v_ref[:, at], d_out, ((1,), (1,))), query, d_out

    ready = products(*jobs[0])
    d_key = d_value = d_query = None
    for i, (p, h) in enumerate(jobs):
        scores, d_probs, query, d_out = ready
        if i + 1 < len(jobs):
            ready = products(*jobs[i + 1])
        at = slice(p * LANES, (p + 1) * LANES)
        probs = jnp.exp2(scores * factor - lse_ref[p, 4 * h : 4 * h + 1, :])
        d_scores = (probs * (d_probs - delta_acc[p, h : h + 1, :])).astype(BF)
        key = k_ref[:, at]
        key = jnp.where(lane // half == h, key, jnp.zeros_like(key))
        terms = (
            dot(probs.astype(BF), d_out),
            dot(d_scores, query),
            dot(d_scores, key, ((0,), (0,))),
        )
        if h == 0:
            d_value, d_key, d_query = terms
            continue
        d_value, d_key, d_query = d_value + terms[0], d_key + terms[1], d_query + terms[2]
        dk_ref[:, at] = (d_key * scale).astype(BF)
        dv_ref[:, at] = d_value.astype(BF)
        sv_acc[1:2, at] += jnp.sum(d_value, axis=0, keepdims=True)
        dq_acc[:, at] += d_query

    @pl.when(step == pl.num_programs(1) - 1)
    def _():
        if final:
            whole = dq_acc[...] * scale
            dq_ref[...] = whole.astype(BF)
            sv_acc[0:1] = jnp.sum(whole, axis=0, keepdims=True)
        else:
            dq_ref[...] = dq_acc[...]
        sums_ref[...] = sv_acc[...]


def parity_block(final, i, at):
    return 2 * i + (at[0] if final else 1 - at[0])


def attend_back(
    final, parts, at, deps, before, partial, queries, keys_values, query_hot, d_out, out,
    logsum, scale,
):
    rows, width = queries.shape
    length = keys_values.shape[0]
    lanes = width // parts
    pairs = lanes // LANES
    per_query = pl.BlockSpec((rows, lanes), lambda part, t, at: (0, part))
    per_key = pl.BlockSpec((rows, lanes), lambda part, t, at: (parity_block(final, t, at), part))
    sums = pl.BlockSpec((8, lanes), lambda part, t, at: (0, part))
    operands = [queries, keys_values, keys_values, query_hot, keys_values, d_out, out, logsum]
    operands += partial
    return pl.pallas_call(
        functools.partial(attend_back_kernel, final, scale, pairs, len(deps) + len(before)),
        grid_spec=pltpu.PrefetchScalarGridSpec(
            num_scalar_prefetch=1,
            grid=(parts, length // rows // 2),
            in_specs=[
                per_query,
                per_key,
                pl.BlockSpec(
                    (rows, lanes), lambda part, t, at: (parity_block(final, t, at), parts + part)
                ),
                pl.BlockSpec((rows, LANES), lambda part, t, at: (0, 0)),
                pl.BlockSpec(
                    (rows, LANES),
                    lambda part, t, at: (parity_block(final, t, at), 2 * width // LANES),
                ),
                per_query,
                per_query,
                pl.BlockSpec((pairs, 8, rows), lambda part, t, at: (part, 0, 0)),
            ]
            + [per_query, sums][: len(partial)]
            + [ANYWHERE] * (len(before) + len(deps)),
            out_specs=[per_query, sums, per_key, per_key, whole_spec((8, LANES))],
            scratch_shapes=[
                pltpu.VMEM((rows, lanes), F32),
                pltpu.VMEM((pairs, 8, rows), F32),
                pltpu.VMEM((8, lanes), F32),
            ],
        ),
        out_shape=[
            jax.ShapeDtypeStruct((rows, width), BF if final else F32),
            jax.ShapeDtypeStruct((8, width), F32),
            jax.ShapeDtypeStruct((length, width), BF),
            jax.ShapeDtypeStruct((length, width), BF),
            jax.ShapeDtypeStruct((8, LANES), F32),
        ],
        input_output_aliases={
            1 + len(operands) + i: 4 - len(before) + i for i in range(len(before))
        },
        name="attend_back",
        **params(10 * rows * length * width, 8 * length * width),
    )(at, *operands, *before, *deps)


def projection_kernel(
    skip, core_ref, x_ref, whole_ref, dq_ref, dk_ref, dv_ref, dwo_ref, one_ref, attn_ref, *refs
):
    keep_ref, give_ref = refs[skip:]
    width = x_ref.shape[1]
    half = width // 2

    def write(first_ref, second_ref):
        first_ref[:width] = dot(whole_ref[...], dk_ref[...], ((0,), (0,))).astype(BF)
        second_ref[:width] = dot(whole_ref[...], dv_ref[...], ((0,), (0,))).astype(BF)
        d_w_q = dot(x_ref[...], dq_ref[...], ((0,), (0,))).astype(BF)
        first_ref[width : width + half] = d_w_q[:half]
        second_ref[width : width + half] = d_w_q[half:]
        first_ref[width + half : 2 * width] = dwo_ref[:half]
        second_ref[width + half : 2 * width] = dwo_ref[half:]
        zeros = jnp.zeros((EXTRA - 32, one_ref.shape[1]), F32)
        sums = [one_ref[...], attn_ref[...], zeros]
        first_ref[2 * width :] = jnp.concatenate(sums, axis=0).astype(BF)
        second_ref[2 * width :] = jnp.zeros((EXTRA, one_ref.shape[1]), BF)

    @pl.when(core_ref[0] == 0)
    def _():
        write(keep_ref, give_ref)

    @pl.when(core_ref[0] == 1)
    def _():
        write(give_ref, keep_ref)


def projection(core, inputs, whole, d_query, d_key, d_value, d_w_out, sums_one, sums_attn, deps):
    rows, width = inputs.shape
    length = whole.shape[0]
    tile = 256

    def columns(count):
        return pl.BlockSpec((count, tile), lambda j, _: (0, j))

    shape = jax.ShapeDtypeStruct((2 * width + EXTRA, width), BF)
    return pl.pallas_call(
        functools.partial(projection_kernel, len(deps)),
        grid_spec=pltpu.PrefetchScalarGridSpec(
            num_scalar_prefetch=1,
            grid=(width // tile,),
            in_specs=[
                whole_spec((rows, width)),
                whole_spec((length, width)),
                columns(rows),
                columns(length),
                columns(length),
                columns(width),
                columns(24),
                columns(8),
            ]
            + [ANYWHERE] * len(deps),
            out_specs=[columns(2 * width + EXTRA)] * 2,
        ),
        out_shape=[shape, shape],
        name="projection",
        **params(4 * length * width * width, 8 * length * width),
    )(core, inputs, whole, d_query, d_key, d_value, d_w_out, sums_one, sums_attn, *deps)


def input_kernel(final, skip, at_ref, dk_ref, dv_ref, w_ref, *refs):
    refs = list(refs)
    if final:
        dq_ref, dh1_ref = refs.pop(0), refs.pop(0)
    out_ref = refs[skip]
    width = dk_ref.shape[1]
    step = pl.program_id(0)
    product = dot(dk_ref[...], w_ref[:, width : 2 * width], ((1,), (1,)))
    product = product + dot(dv_ref[...], w_ref[:, 2 * width :], ((1,), (1,)))
    out_ref[0] = product.astype(out_ref.dtype)
    if final:

        @pl.when(parity_block(True, step, at_ref) == at_ref[1])
        def _():
            out_ref[0] += dh1_ref[...] + dot(dq_ref[...], w_ref[:, :width], ((1,), (1,)))


def input_grad(final, at, d_key, d_value, w_qkv, own, deps):
    width = w_qkv.shape[0]
    count = lax.axis_size("seq")
    rows = d_key.shape[0] // count
    half = count // 2
    per_block = pl.BlockSpec((rows, width), lambda i, at: (parity_block(final, i, at), 0))
    return pl.pallas_call(
        functools.partial(input_kernel, final, len(deps)),
        grid_spec=pltpu.PrefetchScalarGridSpec(
            num_scalar_prefetch=1,
            grid=(half,),
            in_specs=[per_block, per_block, whole_spec(w_qkv.shape)]
            + [whole_spec((rows, width))] * len(own)
            + [ANYWHERE] * len(deps),
            out_specs=pl.BlockSpec((1, rows, width), lambda i, _: (i, 0, 0)),
        ),
        out_shape=jax.ShapeDtypeStruct((half, rows, width), F32 if final else BF),
        name="input_grad",
        **params(2 * count * rows * width * width, 4 * count * rows * width),
    )(at, d_key, d_value, w_qkv, *own, *deps)


def normalise(hidden):
    centred = hidden - jnp.mean(hidden, axis=-1, keepdims=True)
    rstd = lax.rsqrt(jnp.mean(centred * centred, axis=-1, keepdims=True) + 1e-05)
    return centred * rstd, rstd


def norm_back(scaled, normed, rstd):
    return rstd * (
        scaled
        - jnp.mean(scaled, axis=-1, keepdims=True)
        - normed * jnp.mean(scaled * normed, axis=-1, keepdims=True)
    )


def column_sum(value):
    return jnp.sum(value, axis=0, keepdims=True)


def gelu_both(value):
    slope = math.sqrt(2.0 / math.pi)
    square = value * value
    bent = jnp.tanh(slope * (value + 0.044715 * (value * square)))
    rise = 0.5 * (1.0 + bent)
    inner = slope * (1.0 + (3.0 * 0.044715) * square)
    return value * rise, rise + (0.5 * value) * (1.0 - bent * bent) * inner


def ffn_kernel(
    chunks, core_ref, o_ref, x_ref, g_ref, wo_ref, up_ref, down_ref, bup_ref, vec_ref,
    out_ref, keep_ref, give_ref, dh2_ref, du_ref, n1_ref, r1_ref, sums_ref,
    y1, low, act, slope, h2, dh2_low,
):
    step = pl.program_id(0)
    b_out, gain1, bias1, b_down, gain2, bias2 = (vec_ref[i : i + 1] for i in range(6))

    @pl.when(step == 0)
    def _():
        hidden = x_ref[...].astype(F32) + dot(o_ref[...], wo_ref[...]) + b_out
        normed, rstd = normalise(hidden)
        n1_ref[...] = normed
        r1_ref[...] = jnp.broadcast_to(rstd, r1_ref.shape)
        value = normed * gain1 + bias1
        y1[...] = value
        low[...] = value.astype(BF)

    @pl.when(step < chunks)
    def _():
        value, rate = gelu_both(dot(low[...], up_ref[...]) + bup_ref[0])
        act[step] = value.astype(BF)
        slope[step] = rate
        product = dot(act[step], down_ref[...])

        @pl.when(step == 0)
        def _():
            h2[...] = y1[...] + b_down + product

        @pl.when(step > 0)
        def _():
            h2[...] += product

    @pl.when(step == chunks - 1)
    def _():
        normed, rstd = normalise(h2[...])
        out_ref[...] = (normed * gain2 + bias2).astype(BF)
        grad = g_ref[...].astype(F32)
        d_hidden = norm_back(grad * gain2, normed, rstd)
        dh2_ref[...] = d_hidden
        dh2_low[...] = d_hidden.astype(BF)
        sums_ref[...] = jnp.zeros_like(sums_ref)
        sums_ref[0:1] = column_sum(d_hidden)
        sums_ref[1:2] = column_sum(grad * normed)
        sums_ref[2:3] = column_sum(grad)

    @pl.when(step >= chunks)
    def _():
        chunk = 2 * chunks - 1 - step
        d_u = dot(dh2_low[...], down_ref[...], ((1,), (1,))) * slope[chunk]
        sums_ref[pl.ds(8 + chunk, 1)] = column_sum(d_u)
        d_u = d_u.astype(BF)
        du_ref[...] = d_u

        @pl.when(core_ref[0] == 0)
        def _():
            keep_ref[...] = dot(act[chunk], dh2_low[...], ((0,), (0,))).astype(BF)
            give_ref[...] = dot(low[...], d_u, ((0,), (0,))).astype(BF)

        @pl.when(core_ref[0] == 1)
        def _():
            give_ref[...] = dot(act[chunk], dh2_low[...], ((0,), (0,))).astype(BF)
            keep_ref[...] = dot(low[...], d_u, ((0,), (0,))).astype(BF)


def ffn(core, o_low, inputs, grad, w_out, w_up, w_down, b_up, vectors):
    rows, width = inputs.shape
    wide = w_up.shape[1]
    chunks = wide // width
    full = whole_spec

    def fore(i):
        return jnp.minimum(i, chunks - 1)

    def both(i):
        return jnp.where(i < chunks, i, 2 * chunks - 1 - i)

    def back(i):
        return jnp.minimum(2 * chunks - 1 - i, chunks - 1)

    rows_spec = full((rows, width))
    share = pl.BlockSpec((width, width), lambda i, _: (back(i), 0))
    f32_rows = jax.ShapeDtypeStruct((rows, width), F32)
    return pl.pallas_call(
        functools.partial(ffn_kernel, chunks),
        grid_spec=pltpu.PrefetchScalarGridSpec(
            num_scalar_prefetch=1,
            grid=(2 * chunks,),
            in_specs=[
                rows_spec,
                rows_spec,
                rows_spec,
                full((width, width)),
                pl.BlockSpec((width, width), lambda i, _: (0, fore(i))),
                pl.BlockSpec((width, width), lambda i, _: (both(i), 0)),
                pl.BlockSpec((1, 1, width), lambda i, _: (fore(i), 0, 0)),
                full(vectors.shape),
            ],
            out_specs=[
                rows_spec,
                share,
                share,
                rows_spec,
                pl.BlockSpec((rows, width), lambda i, _: (0, back(i))),
                rows_spec,
                full((rows, LANES)),
                full((16, width)),
            ],
            scratch_shapes=[
                pltpu.VMEM((rows, width), F32),
                pltpu.VMEM((rows, width), BF),
                pltpu.VMEM((chunks, rows, width), BF),
                pltpu.VMEM((chunks, rows, width), F32),
                pltpu.VMEM((rows, width), F32),
                pltpu.VMEM((rows, width), BF),
            ],
        ),
        out_shape=[
            jax.ShapeDtypeStruct((rows, width), BF),
            jax.ShapeDtypeStruct((wide, width), BF),
            jax.ShapeDtypeStruct((wide, width), BF),
            f32_rows,
            jax.ShapeDtypeStruct((rows, wide), BF),
            f32_rows,
            jax.ShapeDtypeStruct((rows, LANES), F32),
            jax.ShapeDtypeStruct((16, width), F32),
        ],
        name="ffn",
        **params(11 * rows * width * wide, 12 * width * wide),
    )(core, o_low, inputs, grad, w_out, w_up, w_down, b_up.reshape(chunks, 1, width), vectors)


def norm_one_kernel(
    o_ref, dh2_ref, du_ref, n1_ref, r1_ref, up_ref, wo_ref, gain_ref, two_ref,
    dh1_ref, do_ref, dwo_ref, sums_ref, acc,
):
    step = pl.program_id(0)
    product = dot(du_ref[...], up_ref[...], ((1,), (1,)))

    @pl.when(step == 0)
    def _():
        acc[...] = dh2_ref[...] + product

    @pl.when(step > 0)
    def _():
        acc[...] += product

    @pl.when(step == pl.num_programs(0) - 1)
    def _():
        grad = acc[...]
        normed = n1_ref[...]
        d_hidden = norm_back(grad * gain_ref[0:1], normed, r1_ref[:, 0:1])
        dh1_ref[...] = d_hidden
        low = d_hidden.astype(BF)
        dwo_ref[...] = dot(o_ref[...], low, ((0,), (0,))).astype(BF)
        sums_ref[:16] = two_ref[...]
        sums_ref[16:] = jnp.zeros((8, low.shape[1]), F32)
        sums_ref[16:17] = column_sum(d_hidden)
        sums_ref[17:18] = column_sum(grad * normed)
        sums_ref[18:19] = column_sum(grad)
        do_ref[...] = dot(low, wo_ref[...], ((1,), (1,))).astype(BF)


def norm_one(o_low, dh2, du, n1, r1, w_up, w_out, gain, sums_two):
    rows, width = n1.shape
    wide = w_up.shape[1]
    full = whole_spec
    rows_spec = full((rows, width))
    return pl.pallas_call(
        norm_one_kernel,
        grid=(wide // width,),
        in_specs=[
            rows_spec,
            rows_spec,
            pl.BlockSpec((rows, width), lambda i: (0, i)),
            rows_spec,
            full((rows, LANES)),
            pl.BlockSpec((width, width), lambda i: (0, i)),
            full((width, width)),
            full((1, width)),
            full(sums_two.shape),
        ],
        out_specs=[rows_spec, rows_spec, full((width, width)), full((24, width))],
        out_shape=[
            jax.ShapeDtypeStruct((rows, width), F32),
            jax.ShapeDtypeStruct((rows, width), BF),
            jax.ShapeDtypeStruct((width, width), BF),
            jax.ShapeDtypeStruct((24, width), F32),
        ],
        scratch_shapes=[pltpu.VMEM((rows, width), F32)],
        name="norm_one",
        **params(3 * rows * width * wide, 2 * width * wide),
    )(o_low, dh2, du, n1, r1, w_up, w_out, gain, sums_two)


def place_ffn_kernel(core_ref, mine_ref, other_ref, down_ref, up_ref):
    for core in range(2):

        @pl.when(core_ref[0] == core)
        def _():
            down_ref[...] = (mine_ref, other_ref)[core][...].astype(F32)
            up_ref[...] = (other_ref, mine_ref)[core][...].astype(F32)


def place_ffn(core, wide, mine, other):
    width = mine.shape[1]
    block = pl.BlockSpec((width, width), lambda i, _: (i, 0))
    return pl.pallas_call(
        place_ffn_kernel,
        grid_spec=pltpu.PrefetchScalarGridSpec(
            num_scalar_prefetch=1,
            grid=(wide // width,),
            in_specs=[block, block],
            out_specs=[block, pl.BlockSpec((width, width), lambda i, _: (0, i))],
        ),
        out_shape=[
            jax.ShapeDtypeStruct((wide, width), F32),
            jax.ShapeDtypeStruct((width, wide), F32),
        ],
        name="place_ffn",
        **params(0, 16 * wide * width),
    )(core, mine, other)


def place_attn_kernel(
    core_ref, mine_ref, other_ref, half_mine, half_other, low_mine, low_other,
    out_ref, dwo_ref, small_ref,
):
    half = half_mine.shape[0]
    step = pl.program_id(0)
    for core in range(2):
        mine = core_ref[0] == core

        for at, ref in ((0, out_ref), (1, dwo_ref)):

            @pl.when(jnp.logical_and(mine, step == at))
            def _():
                ref[:half] = (half_mine, half_other)[core][...].astype(F32)
                ref[half:] = (half_other, half_mine)[core][...].astype(F32)

        @pl.when(jnp.logical_and(mine, step == 0))
        def _():
            small_ref[...] = (low_mine, low_other)[core][...].astype(F32)

        for which in range(2):

            @pl.when(jnp.logical_and(mine, step == 1 + which))
            def _():
                out_ref[...] = (mine_ref, other_ref)[(core + which) % 2][...].astype(F32)


def place_attn(core, mine, other):
    width = mine.shape[1]
    half = width // 2
    block = whole_spec((width, width))
    halves = pl.BlockSpec((half, width), lambda i, _: (2 + jnp.minimum(i, 1), 0))
    low = pl.BlockSpec((EXTRA, width), lambda i, _: (2 * width // EXTRA, 0))
    return pl.pallas_call(
        place_attn_kernel,
        grid_spec=pltpu.PrefetchScalarGridSpec(
            num_scalar_prefetch=1,
            grid=(3,),
            in_specs=[block, block, halves, halves, low, low],
            out_specs=[
                pl.BlockSpec((width, width), lambda i, _: (0, i)),
                whole_spec((width, width)),
                whole_spec((EXTRA, width)),
            ],
        ),
        out_shape=[
            jax.ShapeDtypeStruct((width, 3 * width), F32),
            jax.ShapeDtypeStruct((width, width), F32),
            jax.ShapeDtypeStruct((EXTRA, width), F32),
        ],
        name="place_attn",
        **params(0, 24 * width * width),
    )(core, mine, other, mine, other, mine, other)


def per_device(
    layer_input,
    segment_ids,
    w_qkv,
    b_query,
    b_value,
    w_out,
    b_out,
    ln1_gain,
    ln1_bias,
    w_up,
    b_up,
    w_down,
    b_down,
    ln2_gain,
    ln2_bias,
    cotangent,
):
    _, rows, width = layer_input.shape
    scale = (width // HEADS) ** (-0.5)
    inputs = layer_input.reshape(rows, width)
    ids = segment_ids.reshape(rows)

    id_rows = -(-rows // width)
    id_block = jnp.pad(ids.astype(BF), (0, id_rows * width - rows)).reshape(id_rows, width)
    block = jnp.concatenate([inputs, jnp.pad(id_block, ((0, 16 - id_rows), (0, 0)))], axis=0)
    count = lax.axis_size("seq")
    here = lax.axis_index("seq")
    bias = jnp.concatenate([b_query, jnp.zeros_like(b_value), b_value]).reshape(1, -1)
    length = rows * count

    def place(first, second):
        inside = [jnp.logical_and(at >= 0, at < count) for at in (first, second)]
        return jnp.stack(
            [jnp.clip(at, 0, count - 1) for at in (first, second)]
            + [flag.astype(jnp.int32) for flag in inside]
        ).astype(jnp.int32)

    whole, keys_values, queries, query_hot, token = project(
        True, place(here, here), [block], w_qkv, bias, [], length
    )
    ring = line_steps(block)
    way = 1 - 2 * (here & 1)

    def near(k):
        return here + way * k, here - way * k

    for k in range(1, count):
        next(ring)
        pair = ring.send([token])
        whole, keys_values, token = project(
            False, place(*near(k)), pair, w_qkv, bias, [whole, keys_values], length
        )
    attended, attended_low, logsum = attend(queries, keys_values, query_hot, scale)

    core = stages_of("batch")[0]
    core_bit = bit_of(core).reshape(1)
    vectors = jnp.stack([b_out, ln1_gain, ln1_bias, b_down, ln2_gain, ln2_bias] + [b_down] * 2)
    result, kept, give, dh2, du, normed_one, rstd_one, sums_two = ffn(
        core_bit, attended_low, inputs, cotangent.reshape(rows, width),
        w_out, w_up, w_down, b_up, vectors,
    )
    came = swap(give, core)
    d_first, d_attended, d_w_out, sums_one = norm_one(
        attended_low, dh2, du, normed_one, rstd_one, w_up, w_out, ln1_gain.reshape(1, width),
        sums_two,
    )
    came = together([came], [d_first])
    exchanges = Exchanges()
    exchanges.add("ffn", sum_everywhere([kept, *came]))
    here_at = jnp.stack([here & 1, here]).astype(jnp.int32)
    parts = 2

    def back(final, deps, before, partial):
        return attend_back(
            final, parts, here_at, deps, before, partial, queries, keys_values, query_hot,
            d_attended, attended, logsum, scale,
        )

    sent = exchanges.go(["ffn"])
    got = back(False, sent, [], [])
    partial = list(got[:2])
    d_x_sent = input_grad(False, here_at, *got[2:4], w_qkv, [], got[4:])
    exchanges.add("input", line_scatter(d_x_sent))
    sent = exchanges.go(["ffn", "input"], [d_x_sent])
    got = back(True, sent, got[2:4], partial)
    d_query, sums_attn, d_key, d_value, token = got
    sent = exchanges.go(["ffn"], [token])
    attn_kept, attn_give = projection(
        core_bit, inputs, whole, d_query, d_key, d_value, d_w_out, sums_one, sums_attn, sent
    )
    sent = exchanges.go(["ffn"], [attn_kept], land=["input"])
    attn_came = swap(*together([attn_give], sent), core)
    d_x_kept = input_grad(True, here_at, d_key, d_value, w_qkv, [d_query, d_first], sent)
    attn_came = together([attn_came], [d_x_kept])
    exchanges.add("attn", sum_everywhere([attn_kept, *attn_came]))
    both = ["ffn", "attn"]
    exchanges.go(both, [d_x_kept])
    exchanges.go(both)
    exchanges.go(both + ["input"], kept=d_x_kept)
    exchanges.go(both + ["input"])
    exchanges.go(["attn"])
    exchanges.go(["attn"], land=["input"])
    exchanges.go(["attn"], land=["ffn"])
    exchanges.go(["ffn", "input"])
    exchanges.go(["attn"])
    while "ffn" not in exchanges.results:
        exchanges.go(["ffn"])
    d_w_down, d_w_up = place_ffn(core_bit, w_up.shape[1], *exchanges.results["ffn"])
    exchanges.go(["attn"], [d_w_down])
    while len(exchanges.results) < 3:
        exchanges.go(["attn", "input"])
    d_input = exchanges.results["input"]
    d_w_qkv, d_w_out, small = place_attn(core_bit, *exchanges.results["attn"])
    chunks = w_up.shape[1] // width
    d_b_down, d_ln2_gain, d_ln2_bias = (small[i] for i in range(3))
    d_b_up = small[8 : 8 + chunks].reshape(-1)
    d_b_out, d_ln1_gain, d_ln1_bias = (small[16 + i] for i in range(3))
    d_b_query, d_b_value = (small[24 + i] for i in range(2))

    return (
        result.reshape(layer_input.shape),
        d_input.reshape(layer_input.shape),
        d_w_qkv,
        d_b_query,
        d_b_value,
        d_w_out,
        d_b_out,
        d_ln1_gain,
        d_ln1_bias,
        d_w_up,
        d_b_up,
        d_w_down,
        d_b_down,
        d_ln2_gain,
        d_ln2_bias,
    )


def solution(mesh):
    rows = P("batch", "seq", None)
    return jax.shard_map(
        per_device,
        mesh=mesh,
        in_specs=(rows, P("batch", "seq")) + (P(),) * 13 + (rows,),
        out_specs=(rows, rows) + (P(),) * 13,
        check_vma=False,
    )
```

```python
import functools
import math

import jax
import jax.numpy as jnp
from jax import lax
from jax.experimental import pallas as pl
from jax.experimental.pallas import tpu as pltpu
from jax.sharding import PartitionSpec as P

HEADS = 12
LANES = 128
MASK = 1e30
BF = jnp.bfloat16
F32 = jnp.float32
VMEM = 56 * 2**20
EXTRA = 128


def dot(left, right, contract=((1,), (0,))):
    return lax.dot_general(left, right, (contract, ((), ())), preferred_element_type=F32)


def stages_of(axis):
    return [(axis, bit) for bit in range(int(math.log2(lax.axis_size(axis))))]


def bit_of(stage):
    index = lax.axis_index(stage[0])
    if len(stage) == 2:
        return (index >> stage[1]) & 1
    return jnp.where(index % 2 == 0, index >> stage[1], index >> stage[2]) & 1


def swap(value, stage):
    count = lax.axis_size(stage[0])
    bits = stage[1:] * 2
    return lax.ppermute(value, stage[0], [(i, i ^ (1 << bits[i % 2])) for i in range(count)])


ANYWHERE = pl.BlockSpec(memory_space=pl.ANY)


def together(values, late=()):
    if len(values) + len(late) < 2:
        return list(values)
    return pl.pallas_call(
        lambda *refs: None,
        in_specs=[ANYWHERE] * (len(values) + len(late)),
        out_specs=[ANYWHERE] * len(values),
        out_shape=[jax.ShapeDtypeStruct(v.shape, v.dtype) for v in values],
        input_output_aliases={i: i for i in range(len(values))},
        name="together",
    )(*values, *late)


def part_of(terms, index, parts):
    rows = terms[0].shape[0] // parts
    total = lax.dynamic_slice_in_dim(terms[0], index * rows, rows, 0)
    if len(terms) == 1:
        return total
    total = total.astype(F32)
    for term in terms[1:]:
        total = total + lax.dynamic_slice_in_dim(term, index * rows, rows, 0).astype(F32)
    return total.astype(BF)


def rest_of(terms, stage, came):
    mine = bit_of(stage)
    rows = terms[0].shape[0] // 2
    return [lax.dynamic_slice_in_dim(t, mine * rows, rows, 0) for t in terms] + [came]


def total_of(terms):
    total = terms[0].astype(F32)
    for term in terms[1:]:
        total = total + term.astype(F32)
    return total.astype(BF)


def joined(mine, other, stage):
    return jnp.where(
        bit_of(stage) == 0,
        jnp.concatenate([mine, other], axis=0),
        jnp.concatenate([other, mine], axis=0),
    )


def sum_everywhere(terms, merge=False):
    core, chips = stages_of("batch")[0], stages_of("batch")[1:]
    plane = [(axis, one, two) for (axis, one), (_, two) in zip(chips, chips[::-1])]
    line = stages_of("seq")
    order = plane + (line[:-1] if merge else line)
    for stage in order:
        came, _ = yield part_of(terms, 1 - bit_of(stage), 2), stage
        terms = rest_of(terms, stage, came)
    value = total_of(terms)
    if merge:
        came, value = yield value, line[-1]
        value = total_of([value, came])
    for stage in order[:0:-1]:
        came, value = yield value, stage
        value = joined(value, came, stage)
    came, value = yield value, order[0]
    other = swap(value, core)
    other_came, came = yield came, core
    return value, came, other, other_came


def line_scatter(sent):
    stages = stages_of("seq")
    came, kept = yield sent, stages[0]
    for axis, bit in stages[1:]:
        value = kept + came.astype(F32)
        mine = (lax.axis_index(axis) >> bit) & 1
        pairs = value.reshape(value.shape[0] // 2, 2, *value.shape[1:])
        sent = lax.dynamic_index_in_dim(pairs, 1 - mine, 1, keepdims=False).astype(BF)
        kept = lax.dynamic_index_in_dim(pairs, mine, 1, keepdims=False)
        if bit + 1 < len(stages):
            came, _ = yield sent, (axis, bit)
    rows = sent.shape[1]
    came = []
    for begin, end in ((0, rows // 4), (rows // 4, rows // 2), (rows // 2, rows)):
        came.append((yield sent[0, begin:end], stages[-1])[0])
    return kept[0], came


class Exchanges:
    def __init__(self):
        self.chains, self.came, self.sent, self.results = {}, {}, {}, {}
        self.latest = []

    def add(self, name, chain):
        self.chains[name] = chain

    def go(self, names, late=(), kept=None, land=()):
        names = [n for n in names if n not in self.results]
        waiting = [n for n in names if n in self.came]
        landing = waiting + list(land)
        if landing:
            late = list(late) or self.latest
            self.came.update(zip(landing, together([self.came[n] for n in landing], late)))
        next_sent, stages = {}, {}
        for name in names:
            try:
                if name not in waiting:
                    next_sent[name], stages[name] = next(self.chains[name])
                    continue
                back = self.sent[name]
                if name == "input" and kept is not None:
                    back = kept
                next_sent[name], stages[name] = self.chains[name].send((self.came[name], back))
            except StopIteration as stop:
                self.results[name] = stop.value
        next_sent = dict(zip(next_sent, together(list(next_sent.values()))))
        for name, value in next_sent.items():
            self.sent[name], self.came[name] = value, swap(value, stages[name])
        self.latest = list(next_sent.values())
        return self.latest


def line_steps(block):
    count = lax.axis_size("seq")
    pairs = [
        [(i, i ^ 1) for i in range(count)],
        [(i, ((i + 1) ^ 1) - 1) for i in range(1, count - 1)],
    ]
    one = two = block
    for k in range(1, count):
        one, two = lax.ppermute(two, "seq", pairs[0]), lax.ppermute(one, "seq", pairs[1])
        late = yield
        one, two = together([one, two], late)
        yield one, two


def whole_spec(shape):
    return pl.BlockSpec(shape, lambda *_: (0,) * len(shape))


def params(flops, nbytes):
    return dict(
        compiler_params=pltpu.CompilerParams(vmem_limit_bytes=VMEM),
        cost_estimate=pl.CostEstimate(flops=flops, bytes_accessed=nbytes, transcendentals=0),
    )


def hot(ids_row, same, other):
    spread = jnp.broadcast_to(ids_row.astype(F32), (LANES, ids_row.shape[1]))
    lanes = lax.broadcasted_iota(jnp.int32, spread.shape, 0).astype(F32)
    return jnp.transpose(jnp.where(spread == lanes, same, other)).astype(BF)


def project_kernel(first, rows, place_ref, *refs):
    refs = list(refs)
    blocks = [refs.pop(0) for _ in range(1 if first else 2)]
    w_refs = [refs.pop(0) for _ in range(3 if first else 2)]
    b_refs = [refs.pop(0) for _ in range(3 if first else 2)]
    refs = refs if first else refs[2:]
    whole_ref, kv_ref = refs.pop(0), refs.pop(0)
    if first:
        q_ref, qh_ref = refs.pop(0), refs.pop(0)
    token_ref, key_hot, mixed, sems = refs
    token_ref[...] = jnp.zeros_like(token_ref)
    width = blocks[0].shape[1]
    step = pl.program_id(0)
    last = pl.num_programs(0) - 1
    lanes = mixed.shape[-1]

    def valid(b):
        return place_ref[2 + b] == 1

    def block_copies(b):
        at = pl.ds(place_ref[b] * rows, rows)
        return [
            pltpu.make_async_copy(blocks[b].at[pl.ds(0, rows)], whole_ref.at[at], sems.at[b, 0]),
            pltpu.make_async_copy(
                key_hot.at[b], kv_ref.at[at, pl.ds(2 * width, LANES)], sems.at[b, 1]
            ),
        ]

    def step_copies(b, at_step):
        at = pl.ds(place_ref[b] * rows, rows)
        begin = pl.multiple_of(at_step * lanes, LANES)
        return [
            pltpu.make_async_copy(
                mixed.at[b, i, at_step], kv_ref.at[at, pl.ds(i * width + begin, lanes)],
                sems.at[b, 2 + i],
            )
            for i in range(2)
        ]

    for b in range(len(blocks)):

        @pl.when(jnp.logical_and(step == 0, valid(b)))
        def _():
            ids = blocks[b][rows : rows + 16, :rows][0:1]
            key_hot[b] = hot(ids, 0.0, 1.0)
            if first:
                qh_ref[...] = hot(ids, -MASK, 0.0)
            for copy in block_copies(b):
                copy.start()

        @pl.when(valid(b))
        def _():
            block = blocks[b][:rows]
            for i in range(2):
                mixed[b, i, step] = (dot(block, w_refs[i][...]) + b_refs[i][...]).astype(BF)
            if first:
                q_ref[...] = (dot(block, w_refs[2][...]) + b_refs[2][...]).astype(BF)

        @pl.when(jnp.logical_and(step > 0, valid(b)))
        def _():
            for copy in step_copies(b, step - 1):
                copy.wait()

        @pl.when(valid(b))
        def _():
            for copy in step_copies(b, step):
                copy.start()

        @pl.when(jnp.logical_and(step == last, valid(b)))
        def _():
            for copy in step_copies(b, step) + block_copies(b):
                copy.wait()


def project(first, place, blocks, w_qkv, bias, state, length):
    width = w_qkv.shape[0]
    rows = blocks[0].shape[0] - 16
    lanes = 2 * LANES
    steps = width // lanes
    full = whole_spec

    def columns(count, which):
        return pl.BlockSpec((count, lanes), lambda p, *_: (0, which * steps + p))

    parts = (1, 2, 0) if first else (1, 2)
    in_specs = [full(blocks[0].shape)] * len(blocks)
    in_specs += [columns(width, i) for i in parts] + [columns(1, i) for i in parts]
    operands = [*blocks] + [w_qkv] * len(parts) + [bias] * len(parts)
    out_specs = [ANYWHERE, ANYWHERE]
    out_shape = [
        jax.ShapeDtypeStruct((length, width), BF),
        jax.ShapeDtypeStruct((length, 2 * width + LANES), BF),
    ]
    aliases = {}
    if first:
        out_specs += [pl.BlockSpec((rows, lanes), lambda p, *_: (0, p)), full((rows, LANES))]
        out_shape += [
            jax.ShapeDtypeStruct((rows, width), BF),
            jax.ShapeDtypeStruct((rows, LANES), BF),
        ]
    else:
        in_specs += [ANYWHERE, ANYWHERE]
        operands += state
        aliases = {len(operands) - 1: 0, len(operands): 1}
    out_specs.append(full((8, LANES)))
    out_shape.append(jax.ShapeDtypeStruct((8, LANES), F32))
    return pl.pallas_call(
        functools.partial(project_kernel, first, rows),
        grid_spec=pltpu.PrefetchScalarGridSpec(
            num_scalar_prefetch=1,
            grid=(steps,),
            in_specs=in_specs,
            out_specs=out_specs,
            scratch_shapes=[
                pltpu.VMEM((len(blocks), rows, LANES), BF),
                pltpu.VMEM((len(blocks), 2, steps, rows, lanes), BF),
                pltpu.SemaphoreType.DMA((len(blocks), 4)),
            ],
        ),
        out_shape=out_shape,
        input_output_aliases=aliases,
        name="project",
        **params(2 * len(blocks) * rows * width * width, 8 * rows * width),
    )(place, *operands)


def attend_kernel(scale, tile, q_ref, k_ref, v_ref, qh_ref, kh_ref, o_ref, low_ref, lse_ref):
    half = LANES // 2
    lane = lax.broadcasted_iota(jnp.int32, (1, LANES), 1)
    lower = lane < half
    factor = scale * math.log2(math.e)
    jobs = [(t, h) for t in range(q_ref.shape[0] // tile) for h in range(2)]

    def scores_of(t, h):
        at = slice(t * tile, (t + 1) * tile)
        query = q_ref[at]
        query = jnp.where(lane // half == h, query, jnp.zeros_like(query))
        query = jnp.concatenate([query, qh_ref[at]], axis=1)
        return dot(query, jnp.concatenate([k_ref[...], kh_ref[...]], axis=1), ((1,), (1,)))

    ready = scores_of(*jobs[0])
    before = None
    for i, (t, h) in enumerate(jobs):
        scores = ready
        if i + 1 < len(jobs):
            ready = scores_of(*jobs[i + 1])
        peak = jnp.max(scores, axis=1, keepdims=True)
        weights = jnp.exp2((scores - peak) * factor).astype(BF)
        value = v_ref[...]
        both = dot(weights, jnp.concatenate([value, jnp.ones_like(value)], axis=1))
        total = both[:, LANES:]
        now = both[:, :LANES] / total, peak * factor + jnp.log2(total)
        if h == 0:
            before = now
            continue
        at = slice(t * tile, (t + 1) * tile)
        out = jnp.where(lower, before[0], now[0])
        o_ref[at] = out
        low_ref[at] = out.astype(BF)
        turned = jnp.transpose(jnp.where(lower, before[1], now[1]))
        lse_ref[0, :, at] = jnp.concatenate([turned[0:4], turned[half : half + 4]], axis=0)


def attend(queries, keys_values, query_hot, scale):
    rows, width = queries.shape
    length = keys_values.shape[0]
    pairs = width // LANES
    by_pair = pl.BlockSpec((rows, LANES), lambda p: (0, p))
    return pl.pallas_call(
        functools.partial(attend_kernel, scale, 256),
        grid=(pairs,),
        in_specs=[
            by_pair,
            pl.BlockSpec((length, LANES), lambda p: (0, p)),
            pl.BlockSpec((length, LANES), lambda p: (0, pairs + p)),
            pl.BlockSpec((rows, LANES), lambda p: (0, 0)),
            pl.BlockSpec((length, LANES), lambda p: (0, 2 * pairs)),
        ],
        out_specs=[by_pair, by_pair, pl.BlockSpec((1, 8, rows), lambda p: (p, 0, 0))],
        out_shape=[
            jax.ShapeDtypeStruct((rows, width), F32),
            jax.ShapeDtypeStruct((rows, width), BF),
            jax.ShapeDtypeStruct((pairs, 8, rows), F32),
        ],
        name="attend",
        **params(4 * rows * length * width, 8 * length * width),
    )(queries, keys_values, keys_values, query_hot, keys_values)


def attend_back_kernel(
    final, scale, pairs, skip, at_ref, q_ref, k_ref, v_ref, qh_ref, kh_ref, do_ref, o_ref,
    lse_ref, *refs,
):
    refs = list(refs)
    if final:
        dq_in, sums_in = refs.pop(0), refs.pop(0)
    dq_ref, sums_ref, dk_ref, dv_ref, token_ref, dq_acc, delta_acc, sv_acc = refs[skip:]
    step = pl.program_id(1)
    half = LANES // 2
    lane = lax.broadcasted_iota(jnp.int32, (1, LANES), 1)
    factor = scale * math.log2(math.e)
    token_ref[...] = jnp.zeros_like(token_ref)

    @pl.when(step == 0)
    def _():
        if final:
            dq_acc[...] = dq_in[...]
            sv_acc[...] = sums_in[...]
        else:
            dq_acc[...] = jnp.zeros_like(dq_acc)
            sv_acc[...] = jnp.zeros_like(sv_acc)
        for p in range(pairs):
            at = slice(p * LANES, (p + 1) * LANES)
            both = jnp.transpose(do_ref[:, at].astype(F32) * o_ref[:, at])
            delta_acc[p, 0:1] = jnp.sum(both[:half], axis=0, keepdims=True)
            delta_acc[p, 1:2] = jnp.sum(both[half:], axis=0, keepdims=True)

    jobs = [(p, h) for p in range(pairs) for h in range(2)]

    def products(p, h):
        at = slice(p * LANES, (p + 1) * LANES)
        own = lane // half == h
        query, d_out = q_ref[:, at], do_ref[:, at]
        query = jnp.where(own, query, jnp.zeros_like(query))
        d_out = jnp.where(own, d_out, jnp.zeros_like(d_out))
        keys = jnp.concatenate([k_ref[:, at], kh_ref[...]], axis=1)
        scores = dot(keys, jnp.concatenate([query, qh_ref[...]], axis=1), ((1,), (1,)))
        return scores, dot(v_ref[:, at], d_out, ((1,), (1,))), query, d_out

    ready = products(*jobs[0])
    d_key = d_value = d_query = None
    for i, (p, h) in enumerate(jobs):
        scores, d_probs, query, d_out = ready
        if i + 1 < len(jobs):
            ready = products(*jobs[i + 1])
        at = slice(p * LANES, (p + 1) * LANES)
        probs = jnp.exp2(scores * factor - lse_ref[p, 4 * h : 4 * h + 1, :])
        d_scores = (probs * (d_probs - delta_acc[p, h : h + 1, :])).astype(BF)
        key = k_ref[:, at]
        key = jnp.where(lane // half == h, key, jnp.zeros_like(key))
        terms = (
            dot(probs.astype(BF), d_out),
            dot(d_scores, query),
            dot(d_scores, key, ((0,), (0,))),
        )
        if h == 0:
            d_value, d_key, d_query = terms
            continue
        d_value, d_key, d_query = d_value + terms[0], d_key + terms[1], d_query + terms[2]
        dk_ref[:, at] = (d_key * scale).astype(BF)
        dv_ref[:, at] = d_value.astype(BF)
        sv_acc[1:2, at] += jnp.sum(d_value, axis=0, keepdims=True)
        dq_acc[:, at] += d_query

    @pl.when(step == pl.num_programs(1) - 1)
    def _():
        if final:
            whole = dq_acc[...] * scale
            dq_ref[...] = whole.astype(BF)
            sv_acc[0:1] = jnp.sum(whole, axis=0, keepdims=True)
        else:
            dq_ref[...] = dq_acc[...]
        sums_ref[...] = sv_acc[...]


def parity_block(final, i, at):
    return 2 * i + (at[0] if final else 1 - at[0])


def attend_back(
    final, parts, at, deps, before, partial, queries, keys_values, query_hot, d_out, out,
    logsum, scale,
):
    rows, width = queries.shape
    length = keys_values.shape[0]
    lanes = width // parts
    pairs = lanes // LANES
    per_query = pl.BlockSpec((rows, lanes), lambda part, t, at: (0, part))
    per_key = pl.BlockSpec((rows, lanes), lambda part, t, at: (parity_block(final, t, at), part))
    sums = pl.BlockSpec((8, lanes), lambda part, t, at: (0, part))
    operands = [queries, keys_values, keys_values, query_hot, keys_values, d_out, out, logsum]
    operands += partial
    return pl.pallas_call(
        functools.partial(attend_back_kernel, final, scale, pairs, len(deps) + len(before)),
        grid_spec=pltpu.PrefetchScalarGridSpec(
            num_scalar_prefetch=1,
            grid=(parts, length // rows // 2),
            in_specs=[
                per_query,
                per_key,
                pl.BlockSpec(
                    (rows, lanes), lambda part, t, at: (parity_block(final, t, at), parts + part)
                ),
                pl.BlockSpec((rows, LANES), lambda part, t, at: (0, 0)),
                pl.BlockSpec(
                    (rows, LANES),
                    lambda part, t, at: (parity_block(final, t, at), 2 * width // LANES),
                ),
                per_query,
                per_query,
                pl.BlockSpec((pairs, 8, rows), lambda part, t, at: (part, 0, 0)),
            ]
            + [per_query, sums][: len(partial)]
            + [ANYWHERE] * (len(before) + len(deps)),
            out_specs=[per_query, sums, per_key, per_key, whole_spec((8, LANES))],
            scratch_shapes=[
                pltpu.VMEM((rows, lanes), F32),
                pltpu.VMEM((pairs, 8, rows), F32),
                pltpu.VMEM((8, lanes), F32),
            ],
        ),
        out_shape=[
            jax.ShapeDtypeStruct((rows, width), BF if final else F32),
            jax.ShapeDtypeStruct((8, width), F32),
            jax.ShapeDtypeStruct((length, width), BF),
            jax.ShapeDtypeStruct((length, width), BF),
            jax.ShapeDtypeStruct((8, LANES), F32),
        ],
        input_output_aliases={
            1 + len(operands) + i: 4 - len(before) + i for i in range(len(before))
        },
        name="attend_back",
        **params(10 * rows * length * width, 8 * length * width),
    )(at, *operands, *before, *deps)


def projection_kernel(
    skip, core_ref, x_ref, whole_ref, dq_ref, dk_ref, dv_ref, dwo_ref, one_ref, attn_ref, *refs
):
    keep_ref, give_ref = refs[skip:]
    width = x_ref.shape[1]
    half = width // 2

    def write(first_ref, second_ref):
        first_ref[:width] = dot(whole_ref[...], dk_ref[...], ((0,), (0,))).astype(BF)
        second_ref[:width] = dot(whole_ref[...], dv_ref[...], ((0,), (0,))).astype(BF)
        d_w_q = dot(x_ref[...], dq_ref[...], ((0,), (0,))).astype(BF)
        first_ref[width : width + half] = d_w_q[:half]
        second_ref[width : width + half] = d_w_q[half:]
        first_ref[width + half : 2 * width] = dwo_ref[:half]
        second_ref[width + half : 2 * width] = dwo_ref[half:]
        zeros = jnp.zeros((EXTRA - 32, one_ref.shape[1]), F32)
        sums = [one_ref[...], attn_ref[...], zeros]
        first_ref[2 * width :] = jnp.concatenate(sums, axis=0).astype(BF)
        second_ref[2 * width :] = jnp.zeros((EXTRA, one_ref.shape[1]), BF)

    @pl.when(core_ref[0] == 0)
    def _():
        write(keep_ref, give_ref)

    @pl.when(core_ref[0] == 1)
    def _():
        write(give_ref, keep_ref)


def projection(core, inputs, whole, d_query, d_key, d_value, d_w_out, sums_one, sums_attn, deps):
    rows, width = inputs.shape
    length = whole.shape[0]
    tile = 256

    def columns(count):
        return pl.BlockSpec((count, tile), lambda j, _: (0, j))

    shape = jax.ShapeDtypeStruct((2 * width + EXTRA, width), BF)
    return pl.pallas_call(
        functools.partial(projection_kernel, len(deps)),
        grid_spec=pltpu.PrefetchScalarGridSpec(
            num_scalar_prefetch=1,
            grid=(width // tile,),
            in_specs=[
                whole_spec((rows, width)),
                whole_spec((length, width)),
                columns(rows),
                columns(length),
                columns(length),
                columns(width),
                columns(24),
                columns(8),
            ]
            + [ANYWHERE] * len(deps),
            out_specs=[columns(2 * width + EXTRA)] * 2,
        ),
        out_shape=[shape, shape],
        name="projection",
        **params(4 * length * width * width, 8 * length * width),
    )(core, inputs, whole, d_query, d_key, d_value, d_w_out, sums_one, sums_attn, *deps)


def input_kernel(final, skip, at_ref, dk_ref, dv_ref, w_ref, *refs):
    refs = list(refs)
    if final:
        dq_ref, dh1_ref = refs.pop(0), refs.pop(0)
    out_ref = refs[skip]
    width = dk_ref.shape[1]
    step = pl.program_id(0)
    product = dot(dk_ref[...], w_ref[:, width : 2 * width], ((1,), (1,)))
    product = product + dot(dv_ref[...], w_ref[:, 2 * width :], ((1,), (1,)))
    out_ref[0] = product.astype(out_ref.dtype)
    if final:

        @pl.when(parity_block(True, step, at_ref) == at_ref[1])
        def _():
            out_ref[0] += dh1_ref[...] + dot(dq_ref[...], w_ref[:, :width], ((1,), (1,)))


def input_grad(final, at, d_key, d_value, w_qkv, own, deps):
    width = w_qkv.shape[0]
    count = lax.axis_size("seq")
    rows = d_key.shape[0] // count
    half = count // 2
    per_block = pl.BlockSpec((rows, width), lambda i, at: (parity_block(final, i, at), 0))
    return pl.pallas_call(
        functools.partial(input_kernel, final, len(deps)),
        grid_spec=pltpu.PrefetchScalarGridSpec(
            num_scalar_prefetch=1,
            grid=(half,),
            in_specs=[per_block, per_block, whole_spec(w_qkv.shape)]
            + [whole_spec((rows, width))] * len(own)
            + [ANYWHERE] * len(deps),
            out_specs=pl.BlockSpec((1, rows, width), lambda i, _: (i, 0, 0)),
        ),
        out_shape=jax.ShapeDtypeStruct((half, rows, width), F32 if final else BF),
        name="input_grad",
        **params(2 * count * rows * width * width, 4 * count * rows * width),
    )(at, d_key, d_value, w_qkv, *own, *deps)


def normalise(hidden):
    centred = hidden - jnp.mean(hidden, axis=-1, keepdims=True)
    rstd = lax.rsqrt(jnp.mean(centred * centred, axis=-1, keepdims=True) + 1e-05)
    return centred * rstd, rstd


def norm_back(scaled, normed, rstd):
    return rstd * (
        scaled
        - jnp.mean(scaled, axis=-1, keepdims=True)
        - normed * jnp.mean(scaled * normed, axis=-1, keepdims=True)
    )


def column_sum(value):
    return jnp.sum(value, axis=0, keepdims=True)


def gelu_both(value):
    slope = math.sqrt(2.0 / math.pi)
    square = value * value
    bent = jnp.tanh(slope * (value + 0.044715 * (value * square)))
    rise = 0.5 * (1.0 + bent)
    inner = slope * (1.0 + (3.0 * 0.044715) * square)
    return value * rise, rise + (0.5 * value) * (1.0 - bent * bent) * inner


def ffn_kernel(
    chunks, core_ref, o_ref, x_ref, g_ref, wo_ref, up_ref, down_ref, bup_ref, vec_ref,
    out_ref, keep_ref, give_ref, dh2_ref, du_ref, n1_ref, r1_ref, sums_ref,
    y1, low, ahead, act, slope, h2, dh2_low,
):
    step = pl.program_id(0)
    b_out, gain1, bias1, b_down, gain2, bias2 = (vec_ref[i : i + 1] for i in range(6))

    @pl.when(step == 0)
    def _():
        hidden = x_ref[...].astype(F32) + dot(o_ref[...], wo_ref[...]) + b_out
        normed, rstd = normalise(hidden)
        n1_ref[...] = normed
        r1_ref[...] = jnp.broadcast_to(rstd, r1_ref.shape)
        value = normed * gain1 + bias1
        y1[...] = value
        low[...] = value.astype(BF)

    def up_product():
        ahead[step % 2] = dot(low[...], up_ref[...]) + bup_ref[0]

    def down_product():
        value, rate = gelu_both(ahead[(step - 1) % 2])
        value = value.astype(BF)
        act[step - 1] = value
        slope[step - 1] = rate
        h2[...] += dot(value, down_ref[...])

    @pl.when(step == 0)
    def _():
        h2[...] = y1[...] + b_down
        up_product()

    @pl.when(jnp.logical_and(step > 0, step < chunks))
    def _():
        up_product()
        down_product()

    @pl.when(step == chunks)
    def _():
        down_product()
        normed, rstd = normalise(h2[...])
        out_ref[...] = (normed * gain2 + bias2).astype(BF)
        grad = g_ref[...].astype(F32)
        d_hidden = norm_back(grad * gain2, normed, rstd)
        dh2_ref[...] = d_hidden
        dh2_low[...] = d_hidden.astype(BF)
        sums_ref[...] = jnp.zeros_like(sums_ref)
        sums_ref[0:1] = column_sum(d_hidden)
        sums_ref[1:2] = column_sum(grad * normed)
        sums_ref[2:3] = column_sum(grad)

    @pl.when(step > chunks)
    def _():
        chunk = 2 * chunks - step
        d_u = dot(dh2_low[...], down_ref[...], ((1,), (1,))) * slope[chunk]
        sums_ref[pl.ds(8 + chunk, 1)] = column_sum(d_u)
        d_u = d_u.astype(BF)
        du_ref[...] = d_u

        @pl.when(core_ref[0] == 0)
        def _():
            keep_ref[...] = dot(act[chunk], dh2_low[...], ((0,), (0,))).astype(BF)
            give_ref[...] = dot(low[...], d_u, ((0,), (0,))).astype(BF)

        @pl.when(core_ref[0] == 1)
        def _():
            give_ref[...] = dot(act[chunk], dh2_low[...], ((0,), (0,))).astype(BF)
            keep_ref[...] = dot(low[...], d_u, ((0,), (0,))).astype(BF)


def ffn(core, o_low, inputs, grad, w_out, w_up, w_down, b_up, vectors):
    rows, width = inputs.shape
    wide = w_up.shape[1]
    chunks = wide // width
    full = whole_spec

    def fore(i):
        return jnp.minimum(i, chunks - 1)

    def both(i):
        return jnp.where(i <= chunks, jnp.maximum(i - 1, 0), 2 * chunks - i)

    def back(i):
        return jnp.minimum(2 * chunks - i, chunks - 1)

    rows_spec = full((rows, width))
    share = pl.BlockSpec((width, width), lambda i, _: (back(i), 0))
    f32_rows = jax.ShapeDtypeStruct((rows, width), F32)
    return pl.pallas_call(
        functools.partial(ffn_kernel, chunks),
        grid_spec=pltpu.PrefetchScalarGridSpec(
            num_scalar_prefetch=1,
            grid=(2 * chunks + 1,),
            in_specs=[
                rows_spec,
                rows_spec,
                rows_spec,
                full((width, width)),
                pl.BlockSpec((width, width), lambda i, _: (0, fore(i))),
                pl.BlockSpec((width, width), lambda i, _: (both(i), 0)),
                pl.BlockSpec((1, 1, width), lambda i, _: (fore(i), 0, 0)),
                full(vectors.shape),
            ],
            out_specs=[
                rows_spec,
                share,
                share,
                rows_spec,
                pl.BlockSpec((rows, width), lambda i, _: (0, back(i))),
                rows_spec,
                full((rows, LANES)),
                full((16, width)),
            ],
            scratch_shapes=[
                pltpu.VMEM((rows, width), F32),
                pltpu.VMEM((rows, width), BF),
                pltpu.VMEM((2, rows, width), F32),
                pltpu.VMEM((chunks, rows, width), BF),
                pltpu.VMEM((chunks, rows, width), F32),
                pltpu.VMEM((rows, width), F32),
                pltpu.VMEM((rows, width), BF),
            ],
        ),
        out_shape=[
            jax.ShapeDtypeStruct((rows, width), BF),
            jax.ShapeDtypeStruct((wide, width), BF),
            jax.ShapeDtypeStruct((wide, width), BF),
            f32_rows,
            jax.ShapeDtypeStruct((rows, wide), BF),
            f32_rows,
            jax.ShapeDtypeStruct((rows, LANES), F32),
            jax.ShapeDtypeStruct((16, width), F32),
        ],
        name="ffn",
        **params(11 * rows * width * wide, 12 * width * wide),
    )(core, o_low, inputs, grad, w_out, w_up, w_down, b_up.reshape(chunks, 1, width), vectors)


def norm_one_kernel(
    o_ref, dh2_ref, du_ref, n1_ref, r1_ref, up_ref, wo_ref, gain_ref, two_ref,
    dh1_ref, do_ref, dwo_ref, sums_ref, acc,
):
    step = pl.program_id(0)
    product = dot(du_ref[...], up_ref[...], ((1,), (1,)))

    @pl.when(step == 0)
    def _():
        acc[...] = dh2_ref[...] + product

    @pl.when(step > 0)
    def _():
        acc[...] += product

    @pl.when(step == pl.num_programs(0) - 1)
    def _():
        grad = acc[...]
        normed = n1_ref[...]
        d_hidden = norm_back(grad * gain_ref[0:1], normed, r1_ref[:, 0:1])
        dh1_ref[...] = d_hidden
        low = d_hidden.astype(BF)
        dwo_ref[...] = dot(o_ref[...], low, ((0,), (0,))).astype(BF)
        sums_ref[:16] = two_ref[...]
        sums_ref[16:] = jnp.zeros((8, low.shape[1]), F32)
        sums_ref[16:17] = column_sum(d_hidden)
        sums_ref[17:18] = column_sum(grad * normed)
        sums_ref[18:19] = column_sum(grad)
        do_ref[...] = dot(low, wo_ref[...], ((1,), (1,))).astype(BF)


def norm_one(o_low, dh2, du, n1, r1, w_up, w_out, gain, sums_two):
    rows, width = n1.shape
    wide = w_up.shape[1]
    full = whole_spec
    rows_spec = full((rows, width))
    return pl.pallas_call(
        norm_one_kernel,
        grid=(wide // width,),
        in_specs=[
            rows_spec,
            rows_spec,
            pl.BlockSpec((rows, width), lambda i: (0, i)),
            rows_spec,
            full((rows, LANES)),
            pl.BlockSpec((width, width), lambda i: (0, i)),
            full((width, width)),
            full((1, width)),
            full(sums_two.shape),
        ],
        out_specs=[rows_spec, rows_spec, full((width, width)), full((24, width))],
        out_shape=[
            jax.ShapeDtypeStruct((rows, width), F32),
            jax.ShapeDtypeStruct((rows, width), BF),
            jax.ShapeDtypeStruct((width, width), BF),
            jax.ShapeDtypeStruct((24, width), F32),
        ],
        scratch_shapes=[pltpu.VMEM((rows, width), F32)],
        name="norm_one",
        **params(3 * rows * width * wide, 2 * width * wide),
    )(o_low, dh2, du, n1, r1, w_up, w_out, gain, sums_two)


def place_ffn_kernel(at_ref, *refs):
    mine, other, (down_ref, up_ref) = refs[0:2], refs[2:4], refs[4:]
    for late in range(2):
        for core in range(2):

            @pl.when(
                jnp.logical_and(at_ref[0] == core, (pl.program_id(0) >= 2) == bool(late))
            )
            def _():
                down_ref[...] = (mine, other)[core][late][...].astype(F32)
                up_ref[...] = (other, mine)[core][late][...].astype(F32)


def place_ffn(wide, pieces):
    width = pieces[0].shape[1]
    chips = stages_of("batch")[1:]
    bits = [bit_of(stage) for stage in (stages_of("batch")[0], chips[0], chips[-1])]
    early = pl.BlockSpec((width, width), lambda i, _: (jnp.minimum(i, 1), 0))
    late = pl.BlockSpec((width, width), lambda i, _: (jnp.maximum(i - 2, 0), 0))

    def block(i, bit):
        return 2 * jnp.where(i < 2, bit, 1 - bit) + i % 2

    return pl.pallas_call(
        place_ffn_kernel,
        grid_spec=pltpu.PrefetchScalarGridSpec(
            num_scalar_prefetch=1,
            grid=(4,),
            in_specs=[early, late, early, late],
            out_specs=[
                pl.BlockSpec((width, width), lambda i, at: (block(i, at[1]), 0)),
                pl.BlockSpec((width, width), lambda i, at: (0, block(i, at[2]))),
            ],
        ),
        out_shape=[
            jax.ShapeDtypeStruct((wide, width), F32),
            jax.ShapeDtypeStruct((width, wide), F32),
        ],
        name="place_ffn",
        **params(0, 16 * wide * width),
    )(jnp.stack(bits).astype(jnp.int32), *pieces)


def place_attn_kernel(
    at_ref, mine, mine_came, other, other_came, kept_ref, *refs
):
    came, (out_ref, dwo_ref, small_ref, dx_ref) = refs[:-4], refs[-4:]
    width = dwo_ref.shape[0]
    half = width // 2
    rows = mine.shape[0]
    step = pl.program_id(0)

    def part(core, begin, end):
        h = begin // rows
        at = slice(begin - h * rows, end - h * rows)
        own = jnp.where(at_ref[1] == h, mine[at], mine_came[at])
        far = jnp.where(at_ref[2] == h, other[at], other_came[at])
        return jnp.where(at_ref[0] == core, own, far).astype(F32)

    def write(ref, at, core, begin, end):
        cuts = sorted({begin, end} | ({rows} if begin < rows < end else set()))
        for low, high in zip(cuts, cuts[1:]):
            ref[at + low - begin : at + high - begin] = part(core, low, high)

    @pl.when(step == 0)
    def _():
        write(out_ref, 0, 0, width, width + half)
        write(out_ref, half, 1, width, width + half)
        write(small_ref, 0, 0, 2 * width, 2 * width + EXTRA)

    @pl.when(step == 1)
    def _():
        write(out_ref, 0, 0, 0, width)
        write(dwo_ref, 0, 0, width + half, 2 * width)
        write(dwo_ref, half, 1, width + half, 2 * width)

    @pl.when(step == 2)
    def _():
        write(out_ref, 0, 1, 0, width)
        begin = 0
        for ref in came:
            at = slice(begin, begin + ref.shape[0])
            dx_ref[at] = kept_ref[at] + ref[...].astype(F32)
            begin = at.stop


def place_attn(pieces, kept, came):
    width = kept.shape[1]
    chips = stages_of("batch")[1:]
    core, one, two = (bit_of(stage) for stage in (stages_of("batch")[0], chips[0], chips[-1]))
    at = jnp.stack([core, jnp.where(core == 0, one, two), jnp.where(core == 0, two, one)])
    operands = [*pieces, kept, *came]
    return pl.pallas_call(
        place_attn_kernel,
        grid_spec=pltpu.PrefetchScalarGridSpec(
            num_scalar_prefetch=1,
            grid=(3,),
            in_specs=[whole_spec(v.shape) for v in operands],
            out_specs=[
                pl.BlockSpec((width, width), lambda i, _: (0, i)),
                whole_spec((width, width)),
                whole_spec((EXTRA, width)),
                whole_spec(kept.shape),
            ],
        ),
        out_shape=[
            jax.ShapeDtypeStruct((width, 3 * width), F32),
            jax.ShapeDtypeStruct((width, width), F32),
            jax.ShapeDtypeStruct((EXTRA, width), F32),
            jax.ShapeDtypeStruct(kept.shape, F32),
        ],
        name="place_attn",
        **params(0, 24 * width * width),
    )(at.astype(jnp.int32), *operands)


def per_device(
    layer_input,
    segment_ids,
    w_qkv,
    b_query,
    b_value,
    w_out,
    b_out,
    ln1_gain,
    ln1_bias,
    w_up,
    b_up,
    w_down,
    b_down,
    ln2_gain,
    ln2_bias,
    cotangent,
):
    _, rows, width = layer_input.shape
    scale = (width // HEADS) ** (-0.5)
    inputs = layer_input.reshape(rows, width)
    ids = segment_ids.reshape(rows)

    id_rows = -(-rows // width)
    id_block = jnp.pad(ids.astype(BF), (0, id_rows * width - rows)).reshape(id_rows, width)
    block = jnp.concatenate([inputs, jnp.pad(id_block, ((0, 16 - id_rows), (0, 0)))], axis=0)
    count = lax.axis_size("seq")
    here = lax.axis_index("seq")
    bias = jnp.concatenate([b_query, jnp.zeros_like(b_value), b_value]).reshape(1, -1)
    length = rows * count

    def place(first, second):
        inside = [jnp.logical_and(at >= 0, at < count) for at in (first, second)]
        return jnp.stack(
            [jnp.clip(at, 0, count - 1) for at in (first, second)]
            + [flag.astype(jnp.int32) for flag in inside]
        ).astype(jnp.int32)

    whole, keys_values, queries, query_hot, token = project(
        True, place(here, here), [block], w_qkv, bias, [], length
    )
    ring = line_steps(block)
    way = 1 - 2 * (here & 1)

    def near(k):
        return here + way * k, here - way * k

    for k in range(1, count):
        next(ring)
        pair = ring.send([token])
        whole, keys_values, token = project(
            False, place(*near(k)), pair, w_qkv, bias, [whole, keys_values], length
        )
    attended, attended_low, logsum = attend(queries, keys_values, query_hot, scale)

    core = stages_of("batch")[0]
    core_bit = bit_of(core).reshape(1)
    vectors = jnp.stack([b_out, ln1_gain, ln1_bias, b_down, ln2_gain, ln2_bias] + [b_down] * 2)
    result, kept, give, dh2, du, normed_one, rstd_one, sums_two = ffn(
        core_bit, attended_low, inputs, cotangent.reshape(rows, width),
        w_out, w_up, w_down, b_up, vectors,
    )
    came = swap(give, core)
    d_first, d_attended, d_w_out, sums_one = norm_one(
        attended_low, dh2, du, normed_one, rstd_one, w_up, w_out, ln1_gain.reshape(1, width),
        sums_two,
    )
    came = together([came], [d_first])
    exchanges = Exchanges()
    exchanges.add("ffn", sum_everywhere([kept, *came]))
    here_at = jnp.stack([here & 1, here]).astype(jnp.int32)
    parts = 2

    def back(final, deps, before, partial):
        return attend_back(
            final, parts, here_at, deps, before, partial, queries, keys_values, query_hot,
            d_attended, attended, logsum, scale,
        )

    sent = exchanges.go(["ffn"])
    got = back(False, sent, [], [])
    partial = list(got[:2])
    d_x_sent = input_grad(False, here_at, *got[2:4], w_qkv, [], got[4:])
    exchanges.add("input", line_scatter(d_x_sent))
    sent = exchanges.go(["ffn", "input"], [d_x_sent])
    got = back(True, sent, got[2:4], partial)
    d_query, sums_attn, d_key, d_value, token = got
    sent = exchanges.go(["ffn"], [token])
    attn_kept, attn_give = projection(
        core_bit, inputs, whole, d_query, d_key, d_value, d_w_out, sums_one, sums_attn, sent
    )
    sent = exchanges.go(["ffn"], [attn_kept], land=["input"])
    attn_came = swap(*together([attn_give], sent), core)
    d_x_kept = input_grad(True, here_at, d_key, d_value, w_qkv, [d_query, d_first], sent)
    attn_came = together([attn_came], [d_x_kept])
    exchanges.add("attn", sum_everywhere([attn_kept, *attn_came], merge=True))
    both = ["ffn", "attn"]
    exchanges.go(both, [d_x_kept])
    exchanges.go(both)
    exchanges.go(["attn"])
    exchanges.go(["ffn", "input"], kept=d_x_kept)
    exchanges.go(both, land=["input"])
    exchanges.go(["attn"])
    exchanges.go(["attn", "input"], land=["ffn"])
    exchanges.go(["ffn"])
    exchanges.go(["attn", "input"])
    while "ffn" not in exchanges.results:
        exchanges.go(["ffn"])
    d_w_down, d_w_up = place_ffn(w_up.shape[1], exchanges.results["ffn"])
    exchanges.go(["attn"], [d_w_down], land=["input"])
    while len(exchanges.results) < 3:
        exchanges.go(["attn", "input"])
    d_w_qkv, d_w_out, small, d_input = place_attn(
        exchanges.results["attn"], *exchanges.results["input"]
    )
    chunks = w_up.shape[1] // width
    d_b_down, d_ln2_gain, d_ln2_bias = (small[i] for i in range(3))
    d_b_up = small[8 : 8 + chunks].reshape(-1)
    d_b_out, d_ln1_gain, d_ln1_bias = (small[16 + i] for i in range(3))
    d_b_query, d_b_value = (small[24 + i] for i in range(2))

    return (
        result.reshape(layer_input.shape),
        d_input.reshape(layer_input.shape),
        d_w_qkv,
        d_b_query,
        d_b_value,
        d_w_out,
        d_b_out,
        d_ln1_gain,
        d_ln1_bias,
        d_w_up,
        d_b_up,
        d_w_down,
        d_b_down,
        d_ln2_gain,
        d_ln2_bias,
    )


def solution(mesh):
    rows = P("batch", "seq", None)
    return jax.shard_map(
        per_device,
        mesh=mesh,
        in_specs=(rows, P("batch", "seq")) + (P(),) * 13 + (rows,),
        out_specs=(rows, rows) + (P(),) * 13,
        check_vma=False,
    )
```

```python
import functools
import math

import jax
import jax.numpy as jnp
from jax import lax
from jax.experimental import pallas as pl
from jax.experimental.pallas import tpu as pltpu
from jax.sharding import PartitionSpec as P

HEADS = 12
LANES = 128
MASK = 1e30
BF = jnp.bfloat16
F32 = jnp.float32
VMEM = 56 * 2**20
EXTRA = 128


def dot(left, right, contract=((1,), (0,))):
    return lax.dot_general(left, right, (contract, ((), ())), preferred_element_type=F32)


def stages_of(axis):
    return [(axis, bit) for bit in range(int(math.log2(lax.axis_size(axis))))]


def bit_of(stage):
    index = lax.axis_index(stage[0])
    if len(stage) == 2:
        return (index >> stage[1]) & 1
    return jnp.where(index % 2 == 0, index >> stage[1], index >> stage[2]) & 1


def swap(value, stage):
    count = lax.axis_size(stage[0])
    bits = stage[1:] * 2
    return lax.ppermute(value, stage[0], [(i, i ^ (1 << bits[i % 2])) for i in range(count)])


ANYWHERE = pl.BlockSpec(memory_space=pl.ANY)


def together(values, late=()):
    if len(values) + len(late) < 2:
        return list(values)
    return pl.pallas_call(
        lambda *refs: None,
        in_specs=[ANYWHERE] * (len(values) + len(late)),
        out_specs=[ANYWHERE] * len(values),
        out_shape=[jax.ShapeDtypeStruct(v.shape, v.dtype) for v in values],
        input_output_aliases={i: i for i in range(len(values))},
        name="together",
    )(*values, *late)


def part_of(terms, index, parts):
    rows = terms[0].shape[0] // parts
    total = lax.dynamic_slice_in_dim(terms[0], index * rows, rows, 0)
    if len(terms) == 1:
        return total
    total = total.astype(F32)
    for term in terms[1:]:
        total = total + lax.dynamic_slice_in_dim(term, index * rows, rows, 0).astype(F32)
    return total.astype(BF)


def rest_of(terms, stage, came):
    mine = bit_of(stage)
    rows = terms[0].shape[0] // 2
    return [lax.dynamic_slice_in_dim(t, mine * rows, rows, 0) for t in terms] + [came]


def total_of(terms):
    total = terms[0].astype(F32)
    for term in terms[1:]:
        total = total + term.astype(F32)
    return total.astype(BF)


def joined(mine, other, stage):
    return jnp.where(
        bit_of(stage) == 0,
        jnp.concatenate([mine, other], axis=0),
        jnp.concatenate([other, mine], axis=0),
    )


def sum_everywhere(terms, merge=False):
    core, chips = stages_of("batch")[0], stages_of("batch")[1:]
    plane = [(axis, one, two) for (axis, one), (_, two) in zip(chips, chips[::-1])]
    line = stages_of("seq")
    order = plane + (line[:-1] if merge else line)
    for stage in order:
        came, _ = yield part_of(terms, 1 - bit_of(stage), 2), stage
        terms = rest_of(terms, stage, came)
    value = total_of(terms)
    if merge:
        came, value = yield value, line[-1]
        value = total_of([value, came])
    for stage in order[:0:-1]:
        came, value = yield value, stage
        value = joined(value, came, stage)
    came, value = yield value, order[0]
    other = swap(value, core)
    other_came, came = yield came, core
    return value, came, other, other_came


def line_scatter(sent):
    stages = stages_of("seq")
    came, kept = yield sent, stages[0]
    for axis, bit in stages[1:]:
        value = kept + came.astype(F32)
        mine = (lax.axis_index(axis) >> bit) & 1
        pairs = value.reshape(value.shape[0] // 2, 2, *value.shape[1:])
        sent = lax.dynamic_index_in_dim(pairs, 1 - mine, 1, keepdims=False).astype(BF)
        kept = lax.dynamic_index_in_dim(pairs, mine, 1, keepdims=False)
        if bit + 1 < len(stages):
            came, _ = yield sent, (axis, bit)
    rows = sent.shape[1]
    came = []
    for begin, end in ((0, 12), (12, 21), (21, 32)):
        part = sent[0, begin * rows // 32 : end * rows // 32]
        came.append((yield part, stages[-1])[0])
    return kept[0], came


class Exchanges:
    def __init__(self):
        self.chains, self.came, self.sent, self.results = {}, {}, {}, {}
        self.latest = []

    def add(self, name, chain):
        self.chains[name] = chain

    def go(self, names, late=(), kept=None, land=()):
        names = [n for n in names if n not in self.results]
        waiting = [n for n in names if n in self.came]
        landing = waiting + list(land)
        if landing:
            late = list(late) or self.latest
            self.came.update(zip(landing, together([self.came[n] for n in landing], late)))
        next_sent, stages = {}, {}
        for name in names:
            try:
                if name not in waiting:
                    next_sent[name], stages[name] = next(self.chains[name])
                    continue
                back = self.sent[name]
                if name == "input" and kept is not None:
                    back = kept
                next_sent[name], stages[name] = self.chains[name].send((self.came[name], back))
            except StopIteration as stop:
                self.results[name] = stop.value
        next_sent = dict(zip(next_sent, together(list(next_sent.values()))))
        for name, value in next_sent.items():
            self.sent[name], self.came[name] = value, swap(value, stages[name])
        self.latest = list(next_sent.values())
        return self.latest


def line_steps(block):
    count = lax.axis_size("seq")
    pairs = [
        [(i, i ^ 1) for i in range(count)],
        [(i, ((i + 1) ^ 1) - 1) for i in range(1, count - 1)],
    ]
    one = two = block
    for k in range(1, count):
        one, two = lax.ppermute(two, "seq", pairs[0]), lax.ppermute(one, "seq", pairs[1])
        late = yield
        one, two = together([one, two], late)
        yield one, two


def whole_spec(shape):
    return pl.BlockSpec(shape, lambda *_: (0,) * len(shape))


def params(flops, nbytes):
    return dict(
        compiler_params=pltpu.CompilerParams(vmem_limit_bytes=VMEM),
        cost_estimate=pl.CostEstimate(flops=flops, bytes_accessed=nbytes, transcendentals=0),
    )


def hot(ids_row, same, other):
    spread = jnp.broadcast_to(ids_row.astype(F32), (LANES, ids_row.shape[1]))
    lanes = lax.broadcasted_iota(jnp.int32, spread.shape, 0).astype(F32)
    return jnp.transpose(jnp.where(spread == lanes, same, other)).astype(BF)


def project_kernel(first, rows, place_ref, *refs):
    refs = list(refs)
    blocks = [refs.pop(0) for _ in range(1 if first else 2)]
    w_refs = [refs.pop(0) for _ in range(3 if first else 2)]
    b_refs = [refs.pop(0) for _ in range(3 if first else 2)]
    refs = refs if first else refs[2:]
    whole_ref, kv_ref = refs.pop(0), refs.pop(0)
    if first:
        q_ref, qh_ref = refs.pop(0), refs.pop(0)
    token_ref, key_hot, mixed, sems = refs
    token_ref[...] = jnp.zeros_like(token_ref)
    width = blocks[0].shape[1]
    step = pl.program_id(0)
    last = pl.num_programs(0) - 1
    lanes = mixed.shape[-1]

    def valid(b):
        return place_ref[2 + b] == 1

    def block_copies(b):
        at = pl.ds(place_ref[b] * rows, rows)
        return [
            pltpu.make_async_copy(blocks[b].at[pl.ds(0, rows)], whole_ref.at[at], sems.at[b, 0]),
            pltpu.make_async_copy(
                key_hot.at[b], kv_ref.at[at, pl.ds(2 * width, LANES)], sems.at[b, 1]
            ),
        ]

    def step_copies(b, at_step):
        at = pl.ds(place_ref[b] * rows, rows)
        begin = pl.multiple_of(at_step * lanes, LANES)
        return [
            pltpu.make_async_copy(
                mixed.at[b, i, at_step], kv_ref.at[at, pl.ds(i * width + begin, lanes)],
                sems.at[b, 2 + i],
            )
            for i in range(2)
        ]

    for b in range(len(blocks)):

        @pl.when(jnp.logical_and(step == 0, valid(b)))
        def _():
            ids = blocks[b][rows : rows + 16, :rows][0:1]
            key_hot[b] = hot(ids, 0.0, 1.0)
            if first:
                qh_ref[...] = hot(ids, -MASK, 0.0)
            for copy in block_copies(b):
                copy.start()

        @pl.when(valid(b))
        def _():
            block = blocks[b][:rows]
            for i in range(2):
                mixed[b, i, step] = (dot(block, w_refs[i][...]) + b_refs[i][...]).astype(BF)
            if first:
                q_ref[...] = (dot(block, w_refs[2][...]) + b_refs[2][...]).astype(BF)

        @pl.when(jnp.logical_and(step > 0, valid(b)))
        def _():
            for copy in step_copies(b, step - 1):
                copy.wait()

        @pl.when(valid(b))
        def _():
            for copy in step_copies(b, step):
                copy.start()

        @pl.when(jnp.logical_and(step == last, valid(b)))
        def _():
            for copy in step_copies(b, step) + block_copies(b):
                copy.wait()


def project(first, place, blocks, w_qkv, bias, state, length):
    width = w_qkv.shape[0]
    rows = blocks[0].shape[0] - 16
    lanes = 2 * LANES
    steps = width // lanes
    full = whole_spec

    def columns(count, which):
        return pl.BlockSpec((count, lanes), lambda p, *_: (0, which * steps + p))

    parts = (1, 2, 0) if first else (1, 2)
    in_specs = [full(blocks[0].shape)] * len(blocks)
    in_specs += [columns(width, i) for i in parts] + [columns(1, i) for i in parts]
    operands = [*blocks] + [w_qkv] * len(parts) + [bias] * len(parts)
    out_specs = [ANYWHERE, ANYWHERE]
    out_shape = [
        jax.ShapeDtypeStruct((length, width), BF),
        jax.ShapeDtypeStruct((length, 2 * width + LANES), BF),
    ]
    aliases = {}
    if first:
        out_specs += [pl.BlockSpec((rows, lanes), lambda p, *_: (0, p)), full((rows, LANES))]
        out_shape += [
            jax.ShapeDtypeStruct((rows, width), BF),
            jax.ShapeDtypeStruct((rows, LANES), BF),
        ]
    else:
        in_specs += [ANYWHERE, ANYWHERE]
        operands += state
        aliases = {len(operands) - 1: 0, len(operands): 1}
    out_specs.append(full((8, LANES)))
    out_shape.append(jax.ShapeDtypeStruct((8, LANES), F32))
    return pl.pallas_call(
        functools.partial(project_kernel, first, rows),
        grid_spec=pltpu.PrefetchScalarGridSpec(
            num_scalar_prefetch=1,
            grid=(steps,),
            in_specs=in_specs,
            out_specs=out_specs,
            scratch_shapes=[
                pltpu.VMEM((len(blocks), rows, LANES), BF),
                pltpu.VMEM((len(blocks), 2, steps, rows, lanes), BF),
                pltpu.SemaphoreType.DMA((len(blocks), 4)),
            ],
        ),
        out_shape=out_shape,
        input_output_aliases=aliases,
        name="project",
        **params(2 * len(blocks) * rows * width * width, 8 * rows * width),
    )(place, *operands)


def attend_kernel(scale, tile, q_ref, k_ref, v_ref, qh_ref, kh_ref, o_ref, low_ref, lse_ref):
    half = LANES // 2
    lane = lax.broadcasted_iota(jnp.int32, (1, LANES), 1)
    lower = lane < half
    factor = scale * math.log2(math.e)
    jobs = [(t, h) for t in range(q_ref.shape[0] // tile) for h in range(2)]

    def scores_of(t, h):
        at = slice(t * tile, (t + 1) * tile)
        query = q_ref[at]
        query = jnp.where(lane // half == h, query, jnp.zeros_like(query))
        query = jnp.concatenate([query, qh_ref[at]], axis=1)
        return dot(query, jnp.concatenate([k_ref[...], kh_ref[...]], axis=1), ((1,), (1,)))

    ready = scores_of(*jobs[0])
    before = None
    for i, (t, h) in enumerate(jobs):
        scores = ready
        if i + 1 < len(jobs):
            ready = scores_of(*jobs[i + 1])
        peak = jnp.max(scores, axis=1, keepdims=True)
        weights = jnp.exp2((scores - peak) * factor).astype(BF)
        value = v_ref[...]
        both = dot(weights, jnp.concatenate([value, jnp.ones_like(value)], axis=1))
        total = both[:, LANES:]
        now = both[:, :LANES] / total, peak * factor + jnp.log2(total)
        if h == 0:
            before = now
            continue
        at = slice(t * tile, (t + 1) * tile)
        out = jnp.where(lower, before[0], now[0])
        o_ref[at] = out
        low_ref[at] = out.astype(BF)
        turned = jnp.transpose(jnp.where(lower, before[1], now[1]))
        lse_ref[0, :, at] = jnp.concatenate([turned[0:4], turned[half : half + 4]], axis=0)


def attend(queries, keys_values, query_hot, scale):
    rows, width = queries.shape
    length = keys_values.shape[0]
    pairs = width // LANES
    by_pair = pl.BlockSpec((rows, LANES), lambda p: (0, p))
    return pl.pallas_call(
        functools.partial(attend_kernel, scale, 256),
        grid=(pairs,),
        in_specs=[
            by_pair,
            pl.BlockSpec((length, LANES), lambda p: (0, p)),
            pl.BlockSpec((length, LANES), lambda p: (0, pairs + p)),
            pl.BlockSpec((rows, LANES), lambda p: (0, 0)),
            pl.BlockSpec((length, LANES), lambda p: (0, 2 * pairs)),
        ],
        out_specs=[by_pair, by_pair, pl.BlockSpec((1, 8, rows), lambda p: (p, 0, 0))],
        out_shape=[
            jax.ShapeDtypeStruct((rows, width), F32),
            jax.ShapeDtypeStruct((rows, width), BF),
            jax.ShapeDtypeStruct((pairs, 8, rows), F32),
        ],
        name="attend",
        **params(4 * rows * length * width, 8 * length * width),
    )(queries, keys_values, keys_values, query_hot, keys_values)


def attend_back_kernel(
    final, scale, pairs, skip, at_ref, q_ref, k_ref, v_ref, qh_ref, kh_ref, do_ref, o_ref,
    lse_ref, *refs,
):
    refs = list(refs)
    if final:
        dq_in, sums_in = refs.pop(0), refs.pop(0)
    dq_ref, sums_ref, dk_ref, dv_ref, token_ref, dq_acc, delta_acc, sv_acc = refs[skip:]
    step = pl.program_id(1)
    half = LANES // 2
    lane = lax.broadcasted_iota(jnp.int32, (1, LANES), 1)
    factor = scale * math.log2(math.e)
    token_ref[...] = jnp.zeros_like(token_ref)

    @pl.when(step == 0)
    def _():
        if final:
            dq_acc[...] = dq_in[...]
            sv_acc[...] = sums_in[...]
        else:
            dq_acc[...] = jnp.zeros_like(dq_acc)
            sv_acc[...] = jnp.zeros_like(sv_acc)
        for p in range(pairs):
            at = slice(p * LANES, (p + 1) * LANES)
            both = jnp.transpose(do_ref[:, at].astype(F32) * o_ref[:, at])
            delta_acc[p, 0:1] = jnp.sum(both[:half], axis=0, keepdims=True)
            delta_acc[p, 1:2] = jnp.sum(both[half:], axis=0, keepdims=True)

    jobs = [(p, h) for p in range(pairs) for h in range(2)]

    def products(p, h):
        at = slice(p * LANES, (p + 1) * LANES)
        own = lane // half == h
        query, d_out = q_ref[:, at], do_ref[:, at]
        query = jnp.where(own, query, jnp.zeros_like(query))
        d_out = jnp.where(own, d_out, jnp.zeros_like(d_out))
        keys = jnp.concatenate([k_ref[:, at], kh_ref[...]], axis=1)
        scores = dot(keys, jnp.concatenate([query, qh_ref[...]], axis=1), ((1,), (1,)))
        return scores, dot(v_ref[:, at], d_out, ((1,), (1,))), query, d_out

    ready = products(*jobs[0])
    d_key = d_value = d_query = None
    for i, (p, h) in enumerate(jobs):
        scores, d_probs, query, d_out = ready
        if i + 1 < len(jobs):
            ready = products(*jobs[i + 1])
        at = slice(p * LANES, (p + 1) * LANES)
        probs = jnp.exp2(scores * factor - lse_ref[p, 4 * h : 4 * h + 1, :])
        d_scores = (probs * (d_probs - delta_acc[p, h : h + 1, :])).astype(BF)
        key = k_ref[:, at]
        key = jnp.where(lane // half == h, key, jnp.zeros_like(key))
        terms = (
            dot(probs.astype(BF), d_out),
            dot(d_scores, query),
            dot(d_scores, key, ((0,), (0,))),
        )
        if h == 0:
            d_value, d_key, d_query = terms
            continue
        d_value, d_key, d_query = d_value + terms[0], d_key + terms[1], d_query + terms[2]
        dk_ref[:, at] = (d_key * scale).astype(BF)
        dv_ref[:, at] = d_value.astype(BF)
        sv_acc[1:2, at] += jnp.sum(d_value, axis=0, keepdims=True)
        dq_acc[:, at] += d_query

    @pl.when(step == pl.num_programs(1) - 1)
    def _():
        if final:
            whole = dq_acc[...] * scale
            dq_ref[...] = whole.astype(BF)
            sv_acc[0:1] = jnp.sum(whole, axis=0, keepdims=True)
        else:
            dq_ref[...] = dq_acc[...]
        sums_ref[...] = sv_acc[...]


def parity_block(final, i, at):
    return 2 * i + (at[0] if final else 1 - at[0])


def attend_back(
    final, parts, at, deps, before, partial, queries, keys_values, query_hot, d_out, out,
    logsum, scale,
):
    rows, width = queries.shape
    length = keys_values.shape[0]
    lanes = width // parts
    pairs = lanes // LANES
    per_query = pl.BlockSpec((rows, lanes), lambda part, t, at: (0, part))
    per_key = pl.BlockSpec((rows, lanes), lambda part, t, at: (parity_block(final, t, at), part))
    sums = pl.BlockSpec((8, lanes), lambda part, t, at: (0, part))
    operands = [queries, keys_values, keys_values, query_hot, keys_values, d_out, out, logsum]
    operands += partial
    return pl.pallas_call(
        functools.partial(attend_back_kernel, final, scale, pairs, len(deps) + len(before)),
        grid_spec=pltpu.PrefetchScalarGridSpec(
            num_scalar_prefetch=1,
            grid=(parts, length // rows // 2),
            in_specs=[
                per_query,
                per_key,
                pl.BlockSpec(
                    (rows, lanes), lambda part, t, at: (parity_block(final, t, at), parts + part)
                ),
                pl.BlockSpec((rows, LANES), lambda part, t, at: (0, 0)),
                pl.BlockSpec(
                    (rows, LANES),
                    lambda part, t, at: (parity_block(final, t, at), 2 * width // LANES),
                ),
                per_query,
                per_query,
                pl.BlockSpec((pairs, 8, rows), lambda part, t, at: (part, 0, 0)),
            ]
            + [per_query, sums][: len(partial)]
            + [ANYWHERE] * (len(before) + len(deps)),
            out_specs=[per_query, sums, per_key, per_key, whole_spec((8, LANES))],
            scratch_shapes=[
                pltpu.VMEM((rows, lanes), F32),
                pltpu.VMEM((pairs, 8, rows), F32),
                pltpu.VMEM((8, lanes), F32),
            ],
        ),
        out_shape=[
            jax.ShapeDtypeStruct((rows, width), BF if final else F32),
            jax.ShapeDtypeStruct((8, width), F32),
            jax.ShapeDtypeStruct((length, width), BF),
            jax.ShapeDtypeStruct((length, width), BF),
            jax.ShapeDtypeStruct((8, LANES), F32),
        ],
        input_output_aliases={
            1 + len(operands) + i: 4 - len(before) + i for i in range(len(before))
        },
        name="attend_back",
        **params(10 * rows * length * width, 8 * length * width),
    )(at, *operands, *before, *deps)


def projection_kernel(
    skip, core_ref, x_ref, whole_ref, dq_ref, dk_ref, dv_ref, dwo_ref, one_ref, attn_ref, *refs
):
    keep_ref, give_ref = refs[skip:]
    width = x_ref.shape[1]
    half = width // 2

    def write(first_ref, second_ref):
        first_ref[:width] = dot(whole_ref[...], dk_ref[...], ((0,), (0,))).astype(BF)
        second_ref[:width] = dot(whole_ref[...], dv_ref[...], ((0,), (0,))).astype(BF)
        d_w_q = dot(x_ref[...], dq_ref[...], ((0,), (0,))).astype(BF)
        first_ref[width : width + half] = d_w_q[:half]
        second_ref[width : width + half] = d_w_q[half:]
        first_ref[width + half : 2 * width] = dwo_ref[:half]
        second_ref[width + half : 2 * width] = dwo_ref[half:]
        zeros = jnp.zeros((EXTRA - 32, one_ref.shape[1]), F32)
        sums = [one_ref[...], attn_ref[...], zeros]
        first_ref[2 * width :] = jnp.concatenate(sums, axis=0).astype(BF)
        second_ref[2 * width :] = jnp.zeros((EXTRA, one_ref.shape[1]), BF)

    @pl.when(core_ref[0] == 0)
    def _():
        write(keep_ref, give_ref)

    @pl.when(core_ref[0] == 1)
    def _():
        write(give_ref, keep_ref)


def projection(core, inputs, whole, d_query, d_key, d_value, d_w_out, sums_one, sums_attn, deps):
    rows, width = inputs.shape
    length = whole.shape[0]
    tile = 256

    def columns(count):
        return pl.BlockSpec((count, tile), lambda j, _: (0, j))

    shape = jax.ShapeDtypeStruct((2 * width + EXTRA, width), BF)
    return pl.pallas_call(
        functools.partial(projection_kernel, len(deps)),
        grid_spec=pltpu.PrefetchScalarGridSpec(
            num_scalar_prefetch=1,
            grid=(width // tile,),
            in_specs=[
                whole_spec((rows, width)),
                whole_spec((length, width)),
                columns(rows),
                columns(length),
                columns(length),
                columns(width),
                columns(24),
                columns(8),
            ]
            + [ANYWHERE] * len(deps),
            out_specs=[columns(2 * width + EXTRA)] * 2,
        ),
        out_shape=[shape, shape],
        name="projection",
        **params(4 * length * width * width, 8 * length * width),
    )(core, inputs, whole, d_query, d_key, d_value, d_w_out, sums_one, sums_attn, *deps)


def input_kernel(final, skip, at_ref, dk_ref, dv_ref, w_ref, *refs):
    refs = list(refs)
    if final:
        dq_ref, dh1_ref = refs.pop(0), refs.pop(0)
    out_ref = refs[skip]
    width = dk_ref.shape[1]
    step = pl.program_id(0)
    product = dot(dk_ref[...], w_ref[:, width : 2 * width], ((1,), (1,)))
    product = product + dot(dv_ref[...], w_ref[:, 2 * width :], ((1,), (1,)))
    out_ref[0] = product.astype(out_ref.dtype)
    if final:

        @pl.when(parity_block(True, step, at_ref) == at_ref[1])
        def _():
            out_ref[0] += dh1_ref[...] + dot(dq_ref[...], w_ref[:, :width], ((1,), (1,)))


def input_grad(final, at, d_key, d_value, w_qkv, own, deps):
    width = w_qkv.shape[0]
    count = lax.axis_size("seq")
    rows = d_key.shape[0] // count
    half = count // 2
    per_block = pl.BlockSpec((rows, width), lambda i, at: (parity_block(final, i, at), 0))
    return pl.pallas_call(
        functools.partial(input_kernel, final, len(deps)),
        grid_spec=pltpu.PrefetchScalarGridSpec(
            num_scalar_prefetch=1,
            grid=(half,),
            in_specs=[per_block, per_block, whole_spec(w_qkv.shape)]
            + [whole_spec((rows, width))] * len(own)
            + [ANYWHERE] * len(deps),
            out_specs=pl.BlockSpec((1, rows, width), lambda i, _: (i, 0, 0)),
        ),
        out_shape=jax.ShapeDtypeStruct((half, rows, width), F32 if final else BF),
        name="input_grad",
        **params(2 * count * rows * width * width, 4 * count * rows * width),
    )(at, d_key, d_value, w_qkv, *own, *deps)


def normalise(hidden):
    centred = hidden - jnp.mean(hidden, axis=-1, keepdims=True)
    rstd = lax.rsqrt(jnp.mean(centred * centred, axis=-1, keepdims=True) + 1e-05)
    return centred * rstd, rstd


def norm_back(scaled, normed, rstd):
    return rstd * (
        scaled
        - jnp.mean(scaled, axis=-1, keepdims=True)
        - normed * jnp.mean(scaled * normed, axis=-1, keepdims=True)
    )


def column_sum(value):
    return jnp.sum(value, axis=0, keepdims=True)


def gelu_both(value):
    slope = math.sqrt(2.0 / math.pi)
    square = value * value
    bent = jnp.tanh(slope * (value + 0.044715 * (value * square)))
    rise = 0.5 * (1.0 + bent)
    inner = slope * (1.0 + (3.0 * 0.044715) * square)
    return value * rise, rise + (0.5 * value) * (1.0 - bent * bent) * inner


def ffn_kernel(
    chunks, core_ref, o_ref, x_ref, g_ref, wo_ref, up_ref, down_ref, bup_ref, vec_ref,
    out_ref, keep_ref, give_ref, dh2_ref, du_ref, n1_ref, r1_ref, sums_ref,
    y1, low, ahead, act, slope, h2, dh2_low,
):
    step = pl.program_id(0)
    b_out, gain1, bias1, b_down, gain2, bias2 = (vec_ref[i : i + 1] for i in range(6))

    @pl.when(step == 0)
    def _():
        hidden = x_ref[...].astype(F32) + dot(o_ref[...], wo_ref[...]) + b_out
        normed, rstd = normalise(hidden)
        n1_ref[...] = normed
        r1_ref[...] = jnp.broadcast_to(rstd, r1_ref.shape)
        value = normed * gain1 + bias1
        y1[...] = value
        low[...] = value.astype(BF)

    def up_product():
        ahead[step % 2] = dot(low[...], up_ref[...]) + bup_ref[0]

    def down_product():
        value, rate = gelu_both(ahead[(step - 1) % 2])
        value = value.astype(BF)
        act[step - 1] = value
        slope[step - 1] = rate
        h2[...] += dot(value, down_ref[...])

    @pl.when(step == 0)
    def _():
        h2[...] = y1[...] + b_down
        up_product()

    @pl.when(jnp.logical_and(step > 0, step < chunks))
    def _():
        up_product()
        down_product()

    @pl.when(step == chunks)
    def _():
        down_product()
        normed, rstd = normalise(h2[...])
        out_ref[...] = (normed * gain2 + bias2).astype(BF)
        grad = g_ref[...].astype(F32)
        d_hidden = norm_back(grad * gain2, normed, rstd)
        dh2_ref[...] = d_hidden
        dh2_low[...] = d_hidden.astype(BF)
        sums_ref[...] = jnp.zeros_like(sums_ref)
        sums_ref[0:1] = column_sum(d_hidden)
        sums_ref[1:2] = column_sum(grad * normed)
        sums_ref[2:3] = column_sum(grad)

    @pl.when(step > chunks)
    def _():
        chunk = 2 * chunks - step
        d_u = dot(dh2_low[...], down_ref[...], ((1,), (1,))) * slope[chunk]
        sums_ref[pl.ds(8 + chunk, 1)] = column_sum(d_u)
        d_u = d_u.astype(BF)
        du_ref[...] = d_u

        @pl.when(core_ref[0] == 0)
        def _():
            keep_ref[...] = dot(act[chunk], dh2_low[...], ((0,), (0,))).astype(BF)
            give_ref[...] = dot(low[...], d_u, ((0,), (0,))).astype(BF)

        @pl.when(core_ref[0] == 1)
        def _():
            give_ref[...] = dot(act[chunk], dh2_low[...], ((0,), (0,))).astype(BF)
            keep_ref[...] = dot(low[...], d_u, ((0,), (0,))).astype(BF)


def ffn(core, o_low, inputs, grad, w_out, w_up, w_down, b_up, vectors):
    rows, width = inputs.shape
    wide = w_up.shape[1]
    chunks = wide // width
    full = whole_spec

    def fore(i):
        return jnp.minimum(i, chunks - 1)

    def both(i):
        return jnp.where(i <= chunks, jnp.maximum(i - 1, 0), 2 * chunks - i)

    def back(i):
        return jnp.minimum(2 * chunks - i, chunks - 1)

    rows_spec = full((rows, width))
    share = pl.BlockSpec((width, width), lambda i, _: (back(i), 0))
    f32_rows = jax.ShapeDtypeStruct((rows, width), F32)
    return pl.pallas_call(
        functools.partial(ffn_kernel, chunks),
        grid_spec=pltpu.PrefetchScalarGridSpec(
            num_scalar_prefetch=1,
            grid=(2 * chunks + 1,),
            in_specs=[
                rows_spec,
                rows_spec,
                rows_spec,
                full((width, width)),
                pl.BlockSpec((width, width), lambda i, _: (0, fore(i))),
                pl.BlockSpec((width, width), lambda i, _: (both(i), 0)),
                pl.BlockSpec((1, 1, width), lambda i, _: (fore(i), 0, 0)),
                full(vectors.shape),
            ],
            out_specs=[
                rows_spec,
                share,
                share,
                rows_spec,
                pl.BlockSpec((rows, width), lambda i, _: (0, back(i))),
                rows_spec,
                full((rows, LANES)),
                full((16, width)),
            ],
            scratch_shapes=[
                pltpu.VMEM((rows, width), F32),
                pltpu.VMEM((rows, width), BF),
                pltpu.VMEM((2, rows, width), F32),
                pltpu.VMEM((chunks, rows, width), BF),
                pltpu.VMEM((chunks, rows, width), F32),
                pltpu.VMEM((rows, width), F32),
                pltpu.VMEM((rows, width), BF),
            ],
        ),
        out_shape=[
            jax.ShapeDtypeStruct((rows, width), BF),
            jax.ShapeDtypeStruct((wide, width), BF),
            jax.ShapeDtypeStruct((wide, width), BF),
            f32_rows,
            jax.ShapeDtypeStruct((rows, wide), BF),
            f32_rows,
            jax.ShapeDtypeStruct((rows, LANES), F32),
            jax.ShapeDtypeStruct((16, width), F32),
        ],
        name="ffn",
        **params(11 * rows * width * wide, 12 * width * wide),
    )(core, o_low, inputs, grad, w_out, w_up, w_down, b_up.reshape(chunks, 1, width), vectors)


def norm_one_kernel(
    o_ref, dh2_ref, du_ref, n1_ref, r1_ref, up_ref, wo_ref, gain_ref, two_ref,
    dh1_ref, do_ref, dwo_ref, sums_ref, acc,
):
    step = pl.program_id(0)
    product = dot(du_ref[...], up_ref[...], ((1,), (1,)))

    @pl.when(step == 0)
    def _():
        acc[...] = dh2_ref[...] + product

    @pl.when(step > 0)
    def _():
        acc[...] += product

    @pl.when(step == pl.num_programs(0) - 1)
    def _():
        grad = acc[...]
        normed = n1_ref[...]
        d_hidden = norm_back(grad * gain_ref[0:1], normed, r1_ref[:, 0:1])
        dh1_ref[...] = d_hidden
        low = d_hidden.astype(BF)
        dwo_ref[...] = dot(o_ref[...], low, ((0,), (0,))).astype(BF)
        sums_ref[:16] = two_ref[...]
        sums_ref[16:] = jnp.zeros((8, low.shape[1]), F32)
        sums_ref[16:17] = column_sum(d_hidden)
        sums_ref[17:18] = column_sum(grad * normed)
        sums_ref[18:19] = column_sum(grad)
        do_ref[...] = dot(low, wo_ref[...], ((1,), (1,))).astype(BF)


def norm_one(o_low, dh2, du, n1, r1, w_up, w_out, gain, sums_two):
    rows, width = n1.shape
    wide = w_up.shape[1]
    full = whole_spec
    rows_spec = full((rows, width))
    return pl.pallas_call(
        norm_one_kernel,
        grid=(wide // width,),
        in_specs=[
            rows_spec,
            rows_spec,
            pl.BlockSpec((rows, width), lambda i: (0, i)),
            rows_spec,
            full((rows, LANES)),
            pl.BlockSpec((width, width), lambda i: (0, i)),
            full((width, width)),
            full((1, width)),
            full(sums_two.shape),
        ],
        out_specs=[rows_spec, rows_spec, full((width, width)), full((24, width))],
        out_shape=[
            jax.ShapeDtypeStruct((rows, width), F32),
            jax.ShapeDtypeStruct((rows, width), BF),
            jax.ShapeDtypeStruct((width, width), BF),
            jax.ShapeDtypeStruct((24, width), F32),
        ],
        scratch_shapes=[pltpu.VMEM((rows, width), F32)],
        name="norm_one",
        **params(3 * rows * width * wide, 2 * width * wide),
    )(o_low, dh2, du, n1, r1, w_up, w_out, gain, sums_two)


def place_ffn_kernel(at_ref, *refs):
    mine, other, (down_ref, up_ref) = refs[0:2], refs[2:4], refs[4:]
    for late in range(2):
        for core in range(2):

            @pl.when(
                jnp.logical_and(at_ref[0] == core, (pl.program_id(0) >= 2) == bool(late))
            )
            def _():
                down_ref[...] = (mine, other)[core][late][...].astype(F32)
                up_ref[...] = (other, mine)[core][late][...].astype(F32)


def place_ffn(wide, pieces):
    width = pieces[0].shape[1]
    chips = stages_of("batch")[1:]
    bits = [bit_of(stage) for stage in (stages_of("batch")[0], chips[0], chips[-1])]
    early = pl.BlockSpec((width, width), lambda i, _: (jnp.minimum(i, 1), 0))
    late = pl.BlockSpec((width, width), lambda i, _: (jnp.maximum(i - 2, 0), 0))

    def block(i, bit):
        return 2 * jnp.where(i < 2, bit, 1 - bit) + i % 2

    return pl.pallas_call(
        place_ffn_kernel,
        grid_spec=pltpu.PrefetchScalarGridSpec(
            num_scalar_prefetch=1,
            grid=(4,),
            in_specs=[early, late, early, late],
            out_specs=[
                pl.BlockSpec((width, width), lambda i, at: (block(i, at[1]), 0)),
                pl.BlockSpec((width, width), lambda i, at: (0, block(i, at[2]))),
            ],
        ),
        out_shape=[
            jax.ShapeDtypeStruct((wide, width), F32),
            jax.ShapeDtypeStruct((width, wide), F32),
        ],
        name="place_ffn",
        **params(0, 16 * wide * width),
    )(jnp.stack(bits).astype(jnp.int32), *pieces)


def place_attn_kernel(
    at_ref, mine, mine_came, other, other_came, kept_ref, *refs
):
    came, (out_ref, dwo_ref, small_ref, dx_ref) = refs[:-4], refs[-4:]
    width = dwo_ref.shape[0]
    half = width // 2
    rows = mine.shape[0]
    step = pl.program_id(0)

    def part(core, begin, end):
        h = begin // rows
        at = slice(begin - h * rows, end - h * rows)
        own = jnp.where(at_ref[1] == h, mine[at], mine_came[at])
        far = jnp.where(at_ref[2] == h, other[at], other_came[at])
        return jnp.where(at_ref[0] == core, own, far).astype(F32)

    def write(ref, at, core, begin, end):
        cuts = sorted({begin, end} | ({rows} if begin < rows < end else set()))
        for low, high in zip(cuts, cuts[1:]):
            ref[at + low - begin : at + high - begin] = part(core, low, high)

    @pl.when(step == 0)
    def _():
        write(out_ref, 0, 0, width, width + half)
        write(out_ref, half, 1, width, width + half)
        write(small_ref, 0, 0, 2 * width, 2 * width + EXTRA)

    @pl.when(step == 1)
    def _():
        write(out_ref, 0, 0, 0, width)
        write(dwo_ref, 0, 0, width + half, 2 * width)
        write(dwo_ref, half, 1, width + half, 2 * width)

    @pl.when(step == 2)
    def _():
        write(out_ref, 0, 1, 0, width)
        begin = 0
        for ref in came:
            at = slice(begin, begin + ref.shape[0])
            dx_ref[at] = kept_ref[at] + ref[...].astype(F32)
            begin = at.stop


def place_attn(pieces, kept, came):
    width = kept.shape[1]
    chips = stages_of("batch")[1:]
    core, one, two = (bit_of(stage) for stage in (stages_of("batch")[0], chips[0], chips[-1]))
    at = jnp.stack([core, jnp.where(core == 0, one, two), jnp.where(core == 0, two, one)])
    operands = [*pieces, kept, *came]
    return pl.pallas_call(
        place_attn_kernel,
        grid_spec=pltpu.PrefetchScalarGridSpec(
            num_scalar_prefetch=1,
            grid=(3,),
            in_specs=[whole_spec(v.shape) for v in operands],
            out_specs=[
                pl.BlockSpec((width, width), lambda i, _: (0, i)),
                whole_spec((width, width)),
                whole_spec((EXTRA, width)),
                whole_spec(kept.shape),
            ],
        ),
        out_shape=[
            jax.ShapeDtypeStruct((width, 3 * width), F32),
            jax.ShapeDtypeStruct((width, width), F32),
            jax.ShapeDtypeStruct((EXTRA, width), F32),
            jax.ShapeDtypeStruct(kept.shape, F32),
        ],
        name="place_attn",
        **params(0, 24 * width * width),
    )(at.astype(jnp.int32), *operands)


def per_device(
    layer_input,
    segment_ids,
    w_qkv,
    b_query,
    b_value,
    w_out,
    b_out,
    ln1_gain,
    ln1_bias,
    w_up,
    b_up,
    w_down,
    b_down,
    ln2_gain,
    ln2_bias,
    cotangent,
):
    _, rows, width = layer_input.shape
    scale = (width // HEADS) ** (-0.5)
    inputs = layer_input.reshape(rows, width)
    ids = segment_ids.reshape(rows)

    id_rows = -(-rows // width)
    id_block = jnp.pad(ids.astype(BF), (0, id_rows * width - rows)).reshape(id_rows, width)
    block = jnp.concatenate([inputs, jnp.pad(id_block, ((0, 16 - id_rows), (0, 0)))], axis=0)
    count = lax.axis_size("seq")
    here = lax.axis_index("seq")
    bias = jnp.concatenate([b_query, jnp.zeros_like(b_value), b_value]).reshape(1, -1)
    length = rows * count

    def place(first, second):
        inside = [jnp.logical_and(at >= 0, at < count) for at in (first, second)]
        return jnp.stack(
            [jnp.clip(at, 0, count - 1) for at in (first, second)]
            + [flag.astype(jnp.int32) for flag in inside]
        ).astype(jnp.int32)

    whole, keys_values, queries, query_hot, token = project(
        True, place(here, here), [block], w_qkv, bias, [], length
    )
    ring = line_steps(block)
    way = 1 - 2 * (here & 1)

    def near(k):
        return here + way * k, here - way * k

    for k in range(1, count):
        next(ring)
        pair = ring.send([token])
        whole, keys_values, token = project(
            False, place(*near(k)), pair, w_qkv, bias, [whole, keys_values], length
        )
    attended, attended_low, logsum = attend(queries, keys_values, query_hot, scale)

    core = stages_of("batch")[0]
    core_bit = bit_of(core).reshape(1)
    vectors = jnp.stack([b_out, ln1_gain, ln1_bias, b_down, ln2_gain, ln2_bias] + [b_down] * 2)
    result, kept, give, dh2, du, normed_one, rstd_one, sums_two = ffn(
        core_bit, attended_low, inputs, cotangent.reshape(rows, width),
        w_out, w_up, w_down, b_up, vectors,
    )
    came = swap(give, core)
    d_first, d_attended, d_w_out, sums_one = norm_one(
        attended_low, dh2, du, normed_one, rstd_one, w_up, w_out, ln1_gain.reshape(1, width),
        sums_two,
    )
    came = together([came], [d_first])
    exchanges = Exchanges()
    exchanges.add("ffn", sum_everywhere([kept, *came]))
    here_at = jnp.stack([here & 1, here]).astype(jnp.int32)
    parts = 2

    def back(final, deps, before, partial):
        return attend_back(
            final, parts, here_at, deps, before, partial, queries, keys_values, query_hot,
            d_attended, attended, logsum, scale,
        )

    sent = exchanges.go(["ffn"])
    got = back(False, sent, [], [])
    partial = list(got[:2])
    d_x_sent = input_grad(False, here_at, *got[2:4], w_qkv, [], got[4:])
    exchanges.add("input", line_scatter(d_x_sent))
    sent = exchanges.go(["ffn", "input"], [d_x_sent])
    got = back(True, sent, got[2:4], partial)
    d_query, sums_attn, d_key, d_value, token = got
    sent = exchanges.go(["ffn"], [token])
    attn_kept, attn_give = projection(
        core_bit, inputs, whole, d_query, d_key, d_value, d_w_out, sums_one, sums_attn, sent
    )
    sent = exchanges.go(["ffn"], [attn_kept], land=["input"])
    attn_came = swap(*together([attn_give], sent), core)
    d_x_kept = input_grad(True, here_at, d_key, d_value, w_qkv, [d_query, d_first], sent)
    attn_came = together([attn_came], [d_x_kept])
    exchanges.add("attn", sum_everywhere([attn_kept, *attn_came], merge=True))
    both = ["ffn", "attn"]
    exchanges.go(both, [d_x_kept])
    exchanges.go(both)
    exchanges.go(["attn"])
    exchanges.go(["ffn", "input"], kept=d_x_kept)
    exchanges.go(both, land=["input"])
    exchanges.go(["attn"])
    exchanges.go(["attn", "input"], land=["ffn"])
    exchanges.go(["ffn"])
    exchanges.go(["attn", "input"])
    while "ffn" not in exchanges.results:
        exchanges.go(["ffn"])
    d_w_down, d_w_up = place_ffn(w_up.shape[1], exchanges.results["ffn"])
    exchanges.go(["attn"], [d_w_down], land=["input"])
    while len(exchanges.results) < 3:
        exchanges.go(["attn", "input"])
    d_w_qkv, d_w_out, small, d_input = place_attn(
        exchanges.results["attn"], *exchanges.results["input"]
    )
    chunks = w_up.shape[1] // width
    d_b_down, d_ln2_gain, d_ln2_bias = (small[i] for i in range(3))
    d_b_up = small[8 : 8 + chunks].reshape(-1)
    d_b_out, d_ln1_gain, d_ln1_bias = (small[16 + i] for i in range(3))
    d_b_query, d_b_value = (small[24 + i] for i in range(2))

    return (
        result.reshape(layer_input.shape),
        d_input.reshape(layer_input.shape),
        d_w_qkv,
        d_b_query,
        d_b_value,
        d_w_out,
        d_b_out,
        d_ln1_gain,
        d_ln1_bias,
        d_w_up,
        d_b_up,
        d_w_down,
        d_b_down,
        d_ln2_gain,
        d_ln2_bias,
    )


def solution(mesh):
    rows = P("batch", "seq", None)
    return jax.shard_map(
        per_device,
        mesh=mesh,
        in_specs=(rows, P("batch", "seq")) + (P(),) * 13 + (rows,),
        out_specs=(rows, rows) + (P(),) * 13,
        check_vma=False,
    )
```
